512 devices in a mesh: slab: 64 (over z, y_hi, core), chaos: 8 (over y_lo, x).
Axes of the slice: x: 4, y: 8 (y_hi: 4, y_lo: 2; y = y_hi * 2 + y_lo), z: 8, core: 2. Of those that a mesh axis runs over, the one named last changes fastest.
Arguments:
- rhs: float32 [120, 64, 8, 128], P('chaos', 'slab'), may hold values from -6 to 6
- guess: float32 [120, 64, 8, 128], P('chaos', 'slab'), may hold values from -6 to 6
- coef: float32 [36, 64, 8, 128], P(None, 'slab'), may hold values from 0.1 to 1
- block_triples: int32 [48, 3], replicated, may hold values from 0 to 7, as said below
- offsets: int32 [9], replicated, may hold values from 0 to 36, as said below
- values: float32 [48, 15, 12, 15], replicated, may hold values from -0.1875 to 0.1875
Outputs:
- solution: float32 [120, 64, 8, 128], P('chaos', 'slab')
- residual: float32 [120, 64, 8, 128], P('chaos', 'slab')
The draws below stay inside these ranges and needn't reach their ends.
Inputs may be any that keep to these rules, and one draw needn't show every extreme that they name: `block_triples`: rows offsets[I] to offsets[I+1]-1 have first entry I, and within one output block the pairs of second and third entries are distinct; third entries are below 3. Each output block has 3 to 6 rows, exactly 6 for some block; blocks 2p and 2p + 1 together have 6 // 2 + 6 rows. Rows from offsets[8] on are zero and unused. offsets[0] = 0, offsets rise by 3 to 6 from block to block, and offsets[8] = 36.
All inputs are finite; a program needn't handle non-finite values.
Results may differ from the reference program's by a relative error of at most 0.0001.
Values sent between devices are 32-bit elements; how exact they have to be, the bound alone decides.
No kernel may reach another device: no remote copies, remote signals or barrier semaphores. Data moves between devices by JAX's collectives and lax.ppermute only.
A program may use at most 64 MiB of HBM per device.

```python
import math
import jax
import jax.numpy as jnp
from jax import lax

NX = 128
NY = 8
MODE_BLK = 15
MODE_BLOCKS = 8
COEF_BLK = 12
COEF_BLOCKS = 3
TMAX = 6
ITERS = 3
MODES = 120
COEF_MODES = 36
NZ = 64
NTRIP = 48


def triple_lists(key):
    count_key, pick_key, pair_key = jax.random.split(jax.random.fold_in(key, 11), 3)
    pair_count = MODE_BLOCKS // 2
    first_counts = jax.random.randint(count_key, (pair_count,), TMAX // 2, TMAX + 1)
    chosen = jax.random.randint(pick_key, (), 0, pair_count)
    first_counts = jnp.where(jnp.arange(pair_count) == chosen, TMAX, first_counts).astype(jnp.int32)
    second_counts = (TMAX // 2 + TMAX - first_counts).astype(jnp.int32)
    counts = jnp.stack([first_counts, second_counts], axis=1).reshape(-1).astype(jnp.int32)
    offsets = jnp.concatenate([jnp.zeros((1,), jnp.int32), jnp.cumsum(counts).astype(jnp.int32)])
    pair_keys = jax.random.split(pair_key, MODE_BLOCKS)

    def one_order(single):
        return jax.random.permutation(single, MODE_BLOCKS * COEF_BLOCKS)
    orders = jax.vmap(one_order)(pair_keys)[:, :TMAX]
    slots = jnp.arange(TMAX)
    block_ids = jnp.broadcast_to(jnp.arange(MODE_BLOCKS)[:, None], (MODE_BLOCKS, TMAX))
    rows = jnp.stack([block_ids, orders // COEF_BLOCKS, orders % COEF_BLOCKS], axis=-1).astype(jnp.int32)
    target = jnp.where(slots[None, :] < counts[:, None], offsets[:-1][:, None] + slots[None, :], MODE_BLOCKS * TMAX)
    table = jnp.zeros((MODE_BLOCKS * TMAX, 3), jnp.int32).at[target.reshape(-1)].set(rows.reshape(-1, 3), mode='drop')
    return (table, offsets)


def draw_block_triples(key, part):
    return triple_lists(key)[0]


def draw_offsets(key, part):
    return triple_lists(key)[1]


def level_of(stream_key, extent, shards, low, largest):
    gain, own = 1.0, jax.random.fold_in(stream_key, 6)
    for axis_at, parts in shards:
        heights = jnp.exp(jax.random.uniform(jax.random.fold_in(own, axis_at), (parts,), jnp.float32, low / len(shards), largest / len(shards)))
        gain = gain * jnp.repeat(heights, extent[axis_at] // parts).reshape([-1 if axis == axis_at else 1 for axis in range(len(extent))])
    return gain


def bell_draw(key, dims, spread, most, cuts=(), kind=jnp.bfloat16):
    loudness = level_of(key, dims, cuts, -0.22, 0.18) if cuts else 1.0
    values = jax.random.normal(key, dims, jnp.float32) * spread * loudness
    return jnp.minimum(jnp.maximum(values, -most), most).astype(kind)


def setup_inputs(seed: int = 0) -> dict:
    arg_keys = jax.random.split(jax.random.key(seed), 7)
    rhs = bell_draw(arg_keys[0], (MODES, NZ, NY, NX), 1.0, 6.0, ((0, 8), (1, 64)), jnp.float32)
    guess = bell_draw(arg_keys[1], (MODES, NZ, NY, NX), 1.0, 6.0, ((0, 8), (1, 64)), jnp.float32)
    coef = jnp.clip(jnp.exp(math.log(1.0) - 2.3025851 * jax.random.uniform(arg_keys[2], (COEF_MODES, NZ, NY, NX), jnp.float32) ** level_of(arg_keys[2], (COEF_MODES, NZ, NY, NX), ((1, 64),), -0.2, 0.2)), 0.1, 1.0)
    block_triples = draw_block_triples(jax.random.fold_in(arg_keys[6], 71), 0)
    offsets = draw_offsets(jax.random.fold_in(arg_keys[6], 71), 0)
    values = bell_draw(arg_keys[5], (NTRIP, MODE_BLK, COEF_BLK, MODE_BLK), (MODE_BLK * COEF_BLK * TMAX) ** -0.5, 0.1875, (), jnp.float32)
    return {"rhs": rhs, "guess": guess, "coef": coef, "block_triples": block_triples, "offsets": offsets, "values": values}


relax = 0.1


def face_coefs(padded):
    core = padded[:, 1:-1]
    count = padded.shape[0]
    along_x = 0.5 * (core + jnp.roll(core, -1, axis=3))
    along_y = 0.5 * (core + jnp.roll(core, -1, axis=2))
    along_z = 0.5 * (padded[:, :-1] + padded[:, 1:])
    return jnp.concatenate([along_x.reshape(count, -1), along_y.reshape(count, -1), along_z.reshape(count, -1)], axis=1)


def gradients(padded):
    core = padded[:, 1:-1]
    count = padded.shape[0]
    grad_x = jnp.roll(core, -1, axis=3) - core
    grad_y = jnp.roll(core, -1, axis=2) - core
    grad_z = padded[:, 1:] - padded[:, :-1]
    return jnp.concatenate([grad_x.reshape(count, -1), grad_y.reshape(count, -1), grad_z.reshape(count, -1)], axis=1)


def divergence(flux, planes, rows, cols):
    count = flux.shape[0]
    cells = planes * rows * cols
    flux_x = flux[:, :cells].reshape(count, planes, rows, cols)
    flux_y = flux[:, cells:2 * cells].reshape(count, planes, rows, cols)
    flux_z = flux[:, 2 * cells:].reshape(count, planes + 1, rows, cols)
    return (jnp.roll(flux_x, 1, axis=3) - flux_x) + (jnp.roll(flux_y, 1, axis=2) - flux_y) + (flux_z[:, :-1] - flux_z[:, 1:])


def coupling(table, grads_block, coef_block):
    mixed = jnp.dot(table.reshape(-1, table.shape[-1]), grads_block, precision=lax.Precision.HIGHEST, preferred_element_type=jnp.float32)
    mixed = mixed.reshape(table.shape[0], table.shape[1], -1)
    return jnp.sum(mixed * coef_block[None], axis=1)


def apply_operator(field, a_faces, block_triples, offsets, values):
    padded = jnp.pad(field, ((0, 0), (1, 1), (0, 0), (0, 0)))
    grads = gradients(padded)

    def add_triple(index, flux):
        triple = block_triples[index]
        grads_block = lax.dynamic_slice_in_dim(grads, (triple[1] * MODE_BLK).astype(jnp.int32), MODE_BLK, 0)
        coef_block = lax.dynamic_slice_in_dim(a_faces, (triple[2] * COEF_BLK).astype(jnp.int32), COEF_BLK, 0)
        return flux + coupling(values[index], grads_block, coef_block)

    pieces = []
    for block_out in range(MODE_BLOCKS):
        start_flux = jnp.zeros((MODE_BLK, grads.shape[1]), jnp.float32)
        pieces.append(lax.fori_loop(offsets[block_out].astype(jnp.int32), offsets[block_out + 1].astype(jnp.int32), add_triple, start_flux))
    flux = jnp.concatenate(pieces, axis=0)
    return divergence(flux, field.shape[1], field.shape[2], field.shape[3])


def reference(rhs, guess, coef, block_triples, offsets, values):
    a_faces = face_coefs(jnp.pad(coef, ((0, 0), (1, 1), (0, 0), (0, 0))))
    solution = guess
    residual = rhs
    for step in range(ITERS):
        residual = rhs - apply_operator(solution, a_faces, block_triples, offsets, values)
        solution = solution + relax * residual
    return solution, residual
```

```python
import functools

import jax
import jax.numpy as jnp
from jax import lax
from jax.experimental import pallas as pl
from jax.experimental.pallas import tpu as pltpu
from jax.sharding import PartitionSpec as P

MB = 15
MP = 16
NB = 8
CB = 12
NK = 36
KC = 3
NTRIP = 36
ROWS = NB * MP
NX = 128
CP = 40
RELAX = 0.1
f32 = jnp.float32
bf16 = jnp.bfloat16

VM = pl.BlockSpec(memory_space=pltpu.VMEM)
SM = pl.BlockSpec(memory_space=pltpu.SMEM)
PARAMS = pltpu.CompilerParams(vmem_limit_bytes=44 * 2**20)


def call(kernel, outs, ins, scratch=(), specs=None, name=None):
    return pl.pallas_call(
        kernel,
        out_shape=outs,
        in_specs=specs or [VM] * len(ins),
        out_specs=jax.tree.map(lambda _: VM, outs),
        scratch_shapes=scratch,
        compiler_params=PARAMS,
        name=name,
    )(*ins)


def struct(*shape, dtype=f32):
    return jax.ShapeDtypeStruct(shape, dtype)


def table_kernel(trip, values, table, dense, piece):
    dense[...] = jnp.zeros_like(dense)
    piece[...] = jnp.zeros_like(piece)

    def place(t, carry):
        piece[:, :CB, :MB] = values[t]
        block = piece[...].reshape(MB * MP, ROWS)
        block = pltpu.roll(block, trip[t, 1] * MP, 1)
        base = pl.multiple_of((trip[t, 2] * NB + trip[t, 0]) * (MP * MP), MP * MP)
        dense[pl.ds(base, MB * MP), :] += block
        return carry

    lax.fori_loop(0, NTRIP, place, 0)

    for c in range(KC):
        for b in range(NB):
            for k in range(CB):
                x = dense[pl.ds((c * NB + b) * MP * MP + k, MP, stride=MP), :]
                high = x.astype(bf16)
                low = (x - high.astype(f32)).astype(bf16)
                at = pl.ds((c * CB + k) * ROWS + b * MP, MP)
                table[at, 0:128] = high
                table[at, 128:256] = high
                table[at, 256:384] = low


def pack_kernel(guess, rhs, send):
    zero = jnp.zeros((1, NX), f32)
    for y in range(NB):
        g = jnp.concatenate([guess[pl.ds(y, MB, stride=NB), :], zero], axis=0)
        r = jnp.concatenate([rhs[pl.ds(y, MB, stride=NB), :], zero], axis=0)
        for p in range(5):
            send[(y + 2 - p) % NB, p] = g
        for p in range(3):
            send[(y + 1 - p) % NB, 5 + p] = r


def side_kernel(me, got, coef, side, own):
    y = me[0]
    zero = jnp.zeros((CP - NK, NX), f32)
    for q in range(5):
        row = lax.rem(y + q + NB - 2, NB)
        c = jnp.concatenate([coef[pl.ds(row, NK, stride=NB), :], zero], axis=0)
        own[q] = c
        if 1 <= q <= 3:
            side[q - 1, ROWS:, :] = c
            for b in range(NB):
                side[q - 1, b * MP : (b + 1) * MP, :] = got[b, q]


def column(g):
    high = g.astype(bf16)
    low = (g - high.astype(f32)).astype(bf16)
    return jnp.concatenate([high, low, high], axis=0)


def tile_flux(table, grad, weight, extra=None):
    width = grad.shape[1]

    def chunk(c, sums):
        w = jnp.dot(
            table[pl.ds(pl.multiple_of(c * CB * ROWS, CB * ROWS), CB * ROWS), :],
            grad[...],
            preferred_element_type=f32,
        )
        main, more = sums
        for k in range(CB):
            part = w[k * ROWS : (k + 1) * ROWS, :]
            main = main + weight[c, k : k + 1, :] * part
            if extra is not None:
                more = more + extra[c, k : k + 1, :] * part[:, NX:]
        return main, more

    zero = jnp.zeros((ROWS, width), f32)
    none = jnp.zeros((ROWS, NX), f32) if extra is not None else 0
    main, more = lax.fori_loop(0, KC, chunk, (zero, none))
    return main if extra is None else (main, more)


def put_weight(ref, tile, half, a):
    for c in range(KC):
        ref[tile, c, :CB, half * NX : (half + 1) * NX] = a[c * CB : (c + 1) * CB]


def to_right(x):
    return pltpu.roll(x, 1, 1)


def from_right(x):
    return pltpu.roll(x, NX - 1, 1)


def fluxes(table, grad, weight, flux, faces):
    for n, (g, a) in enumerate(faces):
        grad[n // 2, :, (n % 2) * NX : (n % 2 + 1) * NX] = column(g)
        put_weight(weight, n // 2, n % 2, a)
    if len(faces) % 2:
        grad[len(faces) // 2, :, NX:] = jnp.zeros((3 * ROWS, NX), bf16)
        weight[len(faces) // 2, :, :, NX:] = jnp.zeros((KC, MP, NX), f32)

    def tile(n, carry):
        flux[n] = tile_flux(table, grad.at[n], weight.at[n])
        return carry

    lax.fori_loop(0, (len(faces) + 1) // 2, tile, 0)
    return [flux[n // 2, :, (n % 2) * NX : (n % 2 + 1) * NX] for n in range(len(faces))]


def half_sum(a, b):
    return 0.5 * (a + b)


def first_kernel(got, below, above, own, table, three, one, right, grad, weight, flux):
    v = [jnp.concatenate([got[b, p] for b in range(NB)], axis=0) for p in range(5)]
    faces = []
    for r in (1, 2, 3):
        faces.append((from_right(v[r]) - v[r], half_sum(own[r], from_right(own[r]))))
        faces.append((v[r] - below[r - 1, :ROWS], half_sum(below[r - 1, ROWS:], own[r])))
        faces.append((above[r - 1, :ROWS] - v[r], half_sum(own[r], above[r - 1, ROWS:])))
    for r in range(4):
        faces.append((v[r + 1] - v[r], half_sum(own[r], own[r + 1])))
    out = fluxes(table, grad, weight, flux, faces)
    for r in (1, 2, 3):
        fx, low, high = out[3 * (r - 1) : 3 * r]
        image = (to_right(fx) - fx) + (out[9 + r - 1] - out[9 + r]) + (low - high)
        rhs = jnp.concatenate([got[b, 4 + r] for b in range(NB)], axis=0)
        new = v[r] + RELAX * (rhs - image)
        three[r - 1] = new
        if r == 2:
            one[...] = new
            right[...] = rhs


def second_kernel(three, low_v, high_v, below, above, own, right, table, one, grad, weight, flux):
    v = three[1]
    c = own[2]
    faces = [
        (from_right(v) - v, half_sum(c, from_right(c))),
        (v - low_v[...], half_sum(below[1, ROWS:], c)),
        (high_v[...] - v, half_sum(c, above[1, ROWS:])),
        (v - three[0], half_sum(own[1], c)),
        (three[2] - v, half_sum(c, own[3])),
    ]
    fx, zl, zh, yl, yh = fluxes(table, grad, weight, flux, faces)
    image = (to_right(fx) - fx) + (yl - yh) + (zl - zh)
    one[...] = v + RELAX * (right[...] - image)


def third_kernel(mid, low_v, high_v, below, above, own, right, table, send, grad, weight):
    v = mid[...]
    c = own[2]
    columns = [
        (from_right(v) - v, half_sum(c, from_right(c))),
        (v - low_v[...], half_sum(below[1, ROWS:], c)),
        (high_v[...] - v, half_sum(c, above[1, ROWS:])),
        (v, half_sum(c, own[3])),
    ]
    for n, (g, a) in enumerate(columns):
        grad[n // 2, :, (n % 2) * NX : (n % 2 + 1) * NX] = column(g)
        put_weight(weight, n // 2, n % 2, a)
    put_weight(weight, 2, 0, half_sum(own[1], c))
    one = tile_flux(table, grad.at[0], weight.at[0])
    two, y_low = tile_flux(table, grad.at[1], weight.at[1], weight.at[2, :, :, :NX])
    fx, zl = one[:, :NX], one[:, NX:]
    zh, y_high = two[:, :NX], two[:, NX:]
    rest = right[...] - (to_right(fx) - fx) - (zl - zh) - (y_low + y_high)
    for b in range(NB):
        rows = slice(b * MP, (b + 1) * MP)
        send[b, 0] = v[rows]
        send[b, 1] = rest[rows]
        send[b, 2] = y_high[rows]
        send[b, 3] = y_low[rows]


def last_kernel(got, out, residual):
    for y in range(NB):
        res = got[y, 1] + got[(y - 1) % NB, 2] + got[(y + 1) % NB, 3]
        new = got[y, 0] + RELAX * res
        residual[pl.ds(y, MB, stride=NB), :] = res[:MB]
        out[pl.ds(y, MB, stride=NB), :] = new[:MB]


def body(rhs, guess, coef, block_triples, offsets, values):
    slabs = lax.axis_size("slab")
    up = [(i, i + 1) for i in range(slabs - 1)]
    down = [(j, i) for i, j in up]

    def beside(x):
        return lax.ppermute(x, "slab", up), lax.ppermute(x, "slab", down)

    def scratch(tiles, weights):
        return [
            pltpu.VMEM((tiles, 3 * ROWS, 2 * NX), bf16),
            pltpu.VMEM((weights, KC, MP, 2 * NX), f32),
        ]

    me = lax.axis_index("chaos").astype(jnp.int32).reshape(1)
    send = call(
        pack_kernel,
        struct(NB, 8, MP, NX),
        (guess.reshape(MB * NB, NX), rhs.reshape(MB * NB, NX)),
        name="pack",
    )
    got = lax.all_to_all(send, "chaos", 0, 0, tiled=True)
    side, own = call(
        side_kernel,
        (struct(3, ROWS + CP, NX), struct(5, CP, NX)),
        (me, got, coef.reshape(NK * NB, NX)),
        specs=[SM, VM, VM],
        name="side",
    )
    below, above = beside(side)
    table = call(
        table_kernel,
        struct(NK * ROWS, 3 * ROWS, dtype=bf16),
        (block_triples, values),
        scratch=[pltpu.VMEM((KC * NB * MP * MP, ROWS), f32), pltpu.VMEM((MB, MP, ROWS), f32)],
        specs=[SM, VM],
        name="table",
    )
    flat = struct(ROWS, NX)
    three, one, right = call(
        first_kernel,
        (struct(3, ROWS, NX), flat, flat),
        (got, below, above, own, table),
        scratch=scratch(7, 7) + [pltpu.VMEM((7, ROWS, 2 * NX), f32)],
        name="first",
    )
    low_v, high_v = beside(one)
    mid = call(
        second_kernel,
        flat,
        (three, low_v, high_v, below, above, own, right, table),
        scratch=scratch(3, 3) + [pltpu.VMEM((3, ROWS, 2 * NX), f32)],
        name="second",
    )
    low_v, high_v = beside(mid)
    send = call(
        third_kernel,
        struct(NB, 4, MP, NX),
        (mid, low_v, high_v, below, above, own, right, table),
        scratch=scratch(2, 3),
        name="third",
    )
    got = lax.all_to_all(send, "chaos", 0, 0, tiled=True)
    out, residual = call(
        last_kernel, (struct(MB * NB, NX), struct(MB * NB, NX)), (got,), name="last"
    )
    return out.reshape(rhs.shape), residual.reshape(rhs.shape)


def solution(mesh):
    field = P("chaos", "slab", None, None)
    placed = (field, field, P(None, "slab", None, None), P(), P(), P())
    return jax.shard_map(
        body, mesh=mesh, in_specs=placed, out_specs=(field, field), check_vma=False
    )
```

```python
import jax
import jax.numpy as jnp
from jax import lax
from jax.experimental import pallas as pl
from jax.experimental.pallas import tpu as pltpu
from jax.sharding import PartitionSpec as P

MB = 15
MP = 16
NB = 8
CB = 12
KC = 3
NK = 36
NTRIP = 36
ROWS = NB * MP
PART = 4
CHUNK = ROWS // PART
NX = 128
CP = 40
RELAX = 0.1
f32 = jnp.float32
bf16 = jnp.bfloat16

VM = pl.BlockSpec(memory_space=pltpu.VMEM)
SM = pl.BlockSpec(memory_space=pltpu.SMEM)
HBM = pl.BlockSpec(memory_space=pltpu.HBM)
LIMIT = 20 * 2**20
FULL = 60 * 2**20


def call(kernel, name, outs, ins, scratch=(), specs=None, cost=None, limit=LIMIT):
    estimate = None
    if cost is not None:
        estimate = pl.CostEstimate(flops=cost, bytes_accessed=4 * 2**20, transcendentals=0)
    return pl.pallas_call(
        kernel,
        out_shape=outs,
        in_specs=specs or [VM] * len(ins),
        out_specs=jax.tree.map(lambda _: VM, outs),
        scratch_shapes=scratch,
        compiler_params=pltpu.CompilerParams(vmem_limit_bytes=limit),
        cost_estimate=estimate,
        name=name,
    )(*ins)


def struct(*shape, dtype=f32):
    return jax.ShapeDtypeStruct(shape, dtype)


def table_kernel(trip, values, table, dense, piece, turned):
    dense[...] = jnp.zeros_like(dense)
    piece[...] = jnp.zeros_like(piece)
    for half in range(2):
        count = min(8, MB - 8 * half)
        for k in range(CB):
            piece[half, :count, :MB, :] = values[8 * half : 8 * half + count, k]
            block = piece[half].reshape(ROWS, 48)
            turned[half, k * 48 : (k + 1) * 48, :] = block.T

    lane_block = lax.broadcasted_iota(jnp.int32, (CB, ROWS), 1) // MP

    def place(t, carry):
        out, inner, coef = trip[0, t], trip[1, t], trip[2, t]
        base = (out // 2) * (NK * CHUNK) + coef * (CB * CHUNK) + lax.rem(out, 2) * MP
        here = lane_block == inner
        for half in range(2):
            x = turned[half, pl.ds(t, CB, stride=48), :]
            for q in range(8 if half == 0 else MB - 8):
                y = pltpu.roll(x, lax.rem(inner + NB - q, NB) * MP, 1)
                at = pl.ds(base + half * 8 + q, CB, stride=CHUNK)
                dense[at, :] += jnp.where(here, y, 0.0)
        return carry

    lax.fori_loop(0, NTRIP, place, 0)

    def cut(n, carry):
        at = pl.ds(pl.multiple_of(n * ROWS, ROWS), ROWS)
        x = dense[at, :]
        high = x.astype(bf16)
        table[at, 0:128] = high
        table[at, 128:256] = high
        table[at, 256:384] = (x - high.astype(f32)).astype(bf16)
        return carry

    lax.fori_loop(0, NK, cut, 0)


def pack_kernel(me, guess_hbm, rhs_hbm, coef_hbm, send, own, guess, rhs, coef, sem):
    pairs = ((guess_hbm, guess), (rhs_hbm, rhs), (coef_hbm, coef))
    copies = [pltpu.make_async_copy(a, b, sem.at[n]) for n, (a, b) in enumerate(pairs)]
    for copy in copies:
        copy.start()
    zero = jnp.zeros((1, NX), f32)
    copies[0].wait()
    for y in range(NB):
        g = jnp.concatenate([guess[pl.ds(y, MB, stride=NB), :], zero], axis=0)
        for p in range(5):
            send[(y + 2 - p) % NB, p] = g
    copies[1].wait()
    for y in range(NB):
        r = jnp.concatenate([rhs[pl.ds(y, MB, stride=NB), :], zero], axis=0)
        for p in range(3):
            send[(y + 1 - p) % NB, 5 + p] = r
    copies[2].wait()
    for q in range(5):
        row = lax.rem(me[0] + q + NB - 2, NB)
        own[q, :NK] = coef[pl.ds(row, NK, stride=NB), :]
        own[q, NK:] = jnp.zeros((CP - NK, NX), f32)


def side_kernel(got, own, side):
    for q in range(1, 4):
        side[q - 1, ROWS:, :] = own[q]
        for b in range(NB):
            side[q - 1, b * MP : (b + 1) * MP, :] = got[b, q]


def put_columns(grad, tile, columns):
    for n, g in enumerate(columns):
        high = g.astype(bf16)
        low = (g - high.astype(f32)).astype(bf16)
        lanes = slice(n * NX, (n + 1) * NX)
        grad[tile, 0:128, lanes] = high
        grad[tile, 128:256, lanes] = low
        grad[tile, 256:384, lanes] = high


def put_weights(weight, place, halves):
    for n, a in enumerate(halves):
        weight[place, :, n * NX : (n + 1) * NX] = a


def sums(table, grad, tile, width, weight, places):
    rows = []
    for part in range(PART):
        w = jnp.dot(
            table[part * NK * CHUNK : (part + 1) * NK * CHUNK, :],
            grad[tile, :, :width],
            preferred_element_type=f32,
        )
        total = [jnp.zeros((CHUNK, width), f32) for _ in places]
        for k in range(NK):
            here = w[k * CHUNK : (k + 1) * CHUNK]
            for n, p in enumerate(places):
                total[n] = total[n] + weight[p, k : k + 1, :width] * here
        rows.append(total)
    return [jnp.concatenate([r[n] for r in rows], axis=0) for n in range(len(places))]


def to_right(x):
    return pltpu.roll(x, 1, 1)


def from_right(x):
    return pltpu.roll(x, NX - 1, 1)


def mean(a, b):
    return 0.5 * (a + b)


def along_x(plus, minus):
    return minus + plus - to_right(plus) - from_right(minus)


def blocks(got, p):
    return jnp.concatenate([got[b, p] for b in range(NB)], axis=0)


def plane_kernel(got, own, table, base, grad, weight):
    v = [blocks(got, p) for p in range(5)]
    put_columns(grad, 0, [v[1], v[2]])
    put_columns(grad, 1, [v[0], v[4]])
    put_columns(grad, 2, [v[3]])
    ax = [mean(own[r], from_right(own[r])) for r in range(5)]
    ay = [mean(own[r], own[r + 1]) for r in range(4)]
    put_weights(weight, 0, [ax[1], ax[2]])
    put_weights(weight, 1, [to_right(ax[1]), to_right(ax[2])])
    put_weights(weight, 2, [ay[1], ay[2]])
    put_weights(weight, 3, [ay[0], ay[1]])
    put_weights(weight, 4, [ay[0], ay[3]])
    put_weights(weight, 5, [ax[3]])
    put_weights(weight, 6, [to_right(ax[3])])
    put_weights(weight, 7, [ay[3]])
    put_weights(weight, 8, [ay[2]])
    xp, xm, yp, ym = sums(table, grad, 0, 2 * NX, weight, (0, 1, 2, 3))
    (edge,) = sums(table, grad, 1, 2 * NX, weight, (4,))
    xp3, xm3, yp3, ym3 = sums(table, grad, 2, NX, weight, (5, 6, 7, 8))
    plus = [edge[:, :NX], yp[:, :NX], yp[:, NX:], yp3]
    minus = [None, ym[:, :NX], ym[:, NX:], ym3, edge[:, NX:]]
    xs = [None, (xp[:, :NX], xm[:, :NX]), (xp[:, NX:], xm[:, NX:]), (xp3, xm3)]
    for r in (1, 2, 3):
        image = along_x(*xs[r]) + (minus[r] + plus[r] - plus[r - 1] - minus[r + 1])
        base[r - 1] = blocks(got, 4 + r) - image


def put_six(weight, own, low_coef, high_coef):
    c = own[2]
    ax = mean(c, from_right(c))
    six = (ax, to_right(ax), mean(c, own[3]), mean(own[1], c), mean(c, high_coef), mean(low_coef, c))
    for n, a in enumerate(six):
        put_weights(weight, n, [a])


def first_kernel(got, below, above, own, base, table, three, up, down, rest, grad, weight, six):
    for r in range(3):
        v = blocks(got, r + 1)
        put_columns(grad, r, [v - below[r, :ROWS], above[r, :ROWS] - v])
        low, high = mean(below[r, ROWS:], own[r + 1]), mean(own[r + 1], above[r, ROWS:])
        put_weights(weight, r, [low, high])
    put_six(six, own, below[1, ROWS:], above[1, ROWS:])
    for r in range(3):
        (flux,) = sums(table, grad, r, 2 * NX, weight, (r,))
        image = flux[:, :NX] - flux[:, NX:]
        three[r] = blocks(got, r + 1) + RELAX * (base[r] - image)
    put_columns(grad, 3, [three[1]])
    xp, xm, yp, ym, zp, zm = sums(table, grad, 3, NX, six, range(6))
    up[...] = zp
    down[...] = zm
    rest[...] = blocks(got, 6) - along_x(xp, xm) - ((yp + ym) + (zp + zm))


def second_kernel(three, own, table, rest, full, grad, weight):
    put_columns(grad, 0, [three[0], three[2]])
    put_weights(weight, 0, [mean(own[1], own[2]), mean(own[2], own[3])])
    (y,) = sums(table, grad, 0, 2 * NX, weight, (0,))
    full[...] = rest[...] + (y[:, :NX] + y[:, NX:])


def third_kernel(
    three, from_low, from_high, full, got, below, above, own, table, mid, up, down, y_up, y_down, rest, grad, six
):
    v = three[1] + RELAX * (full[...] + (from_low[...] + from_high[...]))
    mid[...] = v
    put_six(six, own, below[1, ROWS:], above[1, ROWS:])
    put_columns(grad, 0, [v])
    xp, xm, yp, ym, zp, zm = sums(table, grad, 0, NX, six, range(6))
    up[...] = zp
    down[...] = zm
    y_up[...] = yp
    y_down[...] = ym
    rest[...] = blocks(got, 6) - along_x(xp, xm) - ((yp + ym) + (zp + zm))


def back_kernel(mid, rest, from_low, from_high, y_up, y_down, send):
    whole = rest[...] + (from_low[...] + from_high[...])
    for b in range(NB):
        rows = slice(b * MP, (b + 1) * MP)
        send[b, 0] = mid[rows]
        send[b, 1] = whole[rows]
        send[b, 2] = y_up[rows]
        send[b, 3] = y_down[rows]


def last_kernel(got, out, residual):
    for y in range(NB):
        res = got[y, 1] + got[(y - 1) % NB, 2] + got[(y + 1) % NB, 3]
        new = got[y, 0] + RELAX * res
        residual[pl.ds(y, MB, stride=NB), :] = res[:MB]
        out[pl.ds(y, MB, stride=NB), :] = new[:MB]


def body(rhs, guess, coef, block_triples, offsets, values):
    slabs = lax.axis_size("slab")
    up = [(i, i + 1) for i in range(slabs - 1)]
    down = [(j, i) for i, j in up]

    def grads(tiles, width=2 * NX):
        return pltpu.VMEM((tiles, 3 * ROWS, width), bf16)

    def weights(count, width=2 * NX):
        return pltpu.VMEM((count, CP, width), f32)

    tile_flops = 2 * NK * ROWS * 3 * ROWS * 2 * NX
    flat = struct(ROWS, NX)
    me = lax.axis_index("chaos").astype(jnp.int32).reshape(1)
    send, own = call(
        pack_kernel,
        "pack",
        (struct(NB, 8, MP, NX), struct(5, CP, NX)),
        (me, guess.reshape(MB * NB, NX), rhs.reshape(MB * NB, NX), coef.reshape(NK * NB, NX)),
        scratch=[
            pltpu.VMEM((MB * NB, NX), f32),
            pltpu.VMEM((MB * NB, NX), f32),
            pltpu.VMEM((NK * NB, NX), f32),
            pltpu.SemaphoreType.DMA((3,)),
        ],
        specs=[SM, HBM, HBM, HBM],
        limit=FULL,
    )
    got = lax.all_to_all(send, "chaos", 0, 0, tiled=True)
    table = call(
        table_kernel,
        "table",
        struct(NK * ROWS, 3 * ROWS, dtype=bf16),
        (block_triples.T, values.transpose(1, 2, 3, 0)),
        scratch=[
            pltpu.VMEM((NK * ROWS, ROWS), f32),
            pltpu.VMEM((2, 8, MP, 48), f32),
            pltpu.VMEM((2, CB * 48, ROWS), f32),
        ],
        specs=[SM, VM],
        cost=6 * tile_flops,
    )
    got, table = lax.optimization_barrier((got, table))
    side = call(side_kernel, "side", struct(3, ROWS + CP, NX), (got, own))
    below = lax.ppermute(side, "slab", up)
    above = lax.ppermute(side, "slab", down)
    base = call(
        plane_kernel,
        "plane",
        struct(3, ROWS, NX),
        (got, own, table),
        scratch=[grads(3), weights(9)],
        cost=3 * tile_flops,
    )
    three, to_up, to_down, rest = call(
        first_kernel,
        "first",
        (struct(3, ROWS, NX), flat, flat, flat),
        (got, below, above, own, base, table),
        scratch=[grads(4), weights(3), weights(6, NX)],
        cost=4 * tile_flops,
    )
    from_low = lax.ppermute(to_up, "slab", up)
    from_high = lax.ppermute(to_down, "slab", down)
    full = call(
        second_kernel,
        "second",
        flat,
        (three, own, table, rest),
        scratch=[grads(1), weights(1)],
        cost=tile_flops,
    )
    mid, to_up, to_down, y_up, y_down, rest = call(
        third_kernel,
        "third",
        (flat,) * 6,
        (three, from_low, from_high, full, got, below, above, own, table),
        scratch=[grads(1, NX), weights(6, NX)],
        cost=tile_flops,
    )
    from_low = lax.ppermute(to_up, "slab", up)
    from_high = lax.ppermute(to_down, "slab", down)
    send = call(
        back_kernel,
        "back",
        struct(NB, 4, MP, NX),
        (mid, rest, from_low, from_high, y_up, y_down),
    )
    got = lax.all_to_all(send, "chaos", 0, 0, tiled=True)
    out, residual = call(
        last_kernel, "last", (struct(MB * NB, NX), struct(MB * NB, NX)), (got,)
    )
    return out.reshape(rhs.shape), residual.reshape(rhs.shape)


def solution(mesh):
    field = P("chaos", "slab", None, None)
    placed = (field, field, P(None, "slab", None, None), P(), P(), P())
    return jax.shard_map(
        body, mesh=mesh, in_specs=placed, out_specs=(field, field), check_vma=False
    )
```

```python
import jax
import jax.numpy as jnp
from jax import lax
from jax.experimental import pallas as pl
from jax.experimental.pallas import tpu as pltpu
from jax.sharding import PartitionSpec as P

MB = 15
MP = 16
NB = 8
CB = 12
KC = 3
NK = 36
NTRIP = 36
LIST = 40
ROWS = NB * MP
PART = 4
CHUNK = ROWS // PART
NX = 128
CP = 40
RELAX = 0.1
f32 = jnp.float32
bf16 = jnp.bfloat16

VM = pl.BlockSpec(memory_space=pltpu.VMEM)
SM = pl.BlockSpec(memory_space=pltpu.SMEM)
ANY = pl.BlockSpec(memory_space=pl.ANY)
HBM = pl.BlockSpec(memory_space=pltpu.HBM)
LIMIT = 20 * 2**20
FULL = 60 * 2**20


def call(kernel, name, outs, ins, scratch=(), specs=None, cost=None, limit=LIMIT):
    estimate = None
    if cost is not None:
        estimate = pl.CostEstimate(flops=cost, bytes_accessed=4 * 2**20, transcendentals=0)
    return pl.pallas_call(
        kernel,
        out_shape=outs,
        in_specs=specs or [VM] * len(ins),
        out_specs=jax.tree.map(lambda _: VM, outs),
        scratch_shapes=scratch,
        compiler_params=pltpu.CompilerParams(vmem_limit_bytes=limit),
        cost_estimate=estimate,
        name=name,
    )(*ins)


def struct(*shape, dtype=f32):
    return jax.ShapeDtypeStruct(shape, dtype)


def table_kernel(trip, values, table, dense, piece, spread):
    dense[...] = jnp.zeros_like(dense)
    piece[...] = jnp.zeros_like(piece)
    first_block = lax.broadcasted_iota(jnp.int32, (LIST, ROWS), 1) < MP
    for half in range(2):
        count = min(8, MB - 8 * half)
        for k in range(CB):
            piece[half, :count, :MB, :] = values[8 * half : 8 * half + count, k]
            block = piece[half].reshape(ROWS, 48).T[:LIST]
            for q in range(8):
                y = pltpu.roll(block, (NB - q) % NB * MP, 1) if q else block
                at = pl.ds(k * LIST * 8 + q, LIST, stride=8)
                spread[half, at, :] = jnp.where(first_block, y, 0.0)

    def place(t, carry):
        out, inner, coef = trip[0, t], trip[1, t], trip[2, t]
        base = (out // 2) * (NK * CHUNK) + coef * (CB * CHUNK) + lax.rem(out, 2) * MP
        for half in range(2):
            for k in range(CB):
                x = spread[half, pl.ds(pl.multiple_of((k * LIST + t) * 8, 8), 8), :]
                at = pl.ds(pl.multiple_of(base + k * CHUNK + half * 8, 8), 8)
                dense[at, :] += pltpu.roll(x, inner * MP, 1)
        return carry

    lax.fori_loop(0, NTRIP, place, 0)

    def cut(n, carry):
        at = pl.ds(pl.multiple_of(n * ROWS, ROWS), ROWS)
        x = dense[at, :]
        high = x.astype(bf16)
        table[at, 0:128] = high
        table[at, 128:256] = high
        table[at, 256:384] = (x - high.astype(f32)).astype(bf16)
        return carry

    lax.fori_loop(0, NK, cut, 0)


def pack_kernel(guess_hbm, rhs_hbm, send, guess, rhs, sem):
    pairs = ((guess_hbm, guess), (rhs_hbm, rhs))
    copies = [pltpu.make_async_copy(a, b, sem.at[n]) for n, (a, b) in enumerate(pairs)]
    for copy in copies:
        copy.start()
    zero = jnp.zeros((1, NX), f32)
    copies[0].wait()
    for y in range(NB):
        g = jnp.concatenate([guess[pl.ds(y, MB, stride=NB), :], zero], axis=0)
        for p in range(5):
            send[(y + 2 - p) % NB, p] = g
    copies[1].wait()
    for y in range(NB):
        r = jnp.concatenate([rhs[pl.ds(y, MB, stride=NB), :], zero], axis=0)
        for p in range(3):
            send[(y + 1 - p) % NB, 5 + p] = r


def side_kernel(me, got, coef, table, side, own, rows):
    del table
    for q in range(5):
        row = lax.rem(me[0] + q + NB - 2, NB)
        c = jnp.concatenate(
            [coef[pl.ds(row, NK, stride=NB), :], jnp.zeros((CP - NK, NX), f32)], axis=0
        )
        own[q] = c
        if 1 <= q <= 3:
            side[q - 1, ROWS:, :] = c
    for q in range(8):
        for b in range(NB):
            x = got[b, q]
            rows[q, b * MP : (b + 1) * MP, :] = x
            if 1 <= q <= 3:
                side[q - 1, b * MP : (b + 1) * MP, :] = x


def put_columns(grad, tile, columns):
    for n, g in enumerate(columns):
        high = g.astype(bf16)
        low = (g - high.astype(f32)).astype(bf16)
        lanes = slice(n * NX, (n + 1) * NX)
        grad[tile, 0:128, lanes] = high
        grad[tile, 128:256, lanes] = low
        grad[tile, 256:384, lanes] = high


def put_weights(weight, place, halves):
    for n, a in enumerate(halves):
        weight[place, :, n * NX : (n + 1) * NX] = a


def sums(table, grad, tile, width, weight, places):
    rows = []
    for part in range(PART):
        w = jnp.dot(
            table[part * NK * CHUNK : (part + 1) * NK * CHUNK, :],
            grad[tile, :, :width],
            preferred_element_type=f32,
        )
        total = [jnp.zeros((CHUNK, width), f32) for _ in places]
        for k in range(NK):
            here = w[k * CHUNK : (k + 1) * CHUNK]
            for n, p in enumerate(places):
                total[n] = total[n] + weight[p, k : k + 1, :width] * here
        rows.append(total)
    return [jnp.concatenate([r[n] for r in rows], axis=0) for n in range(len(places))]


def to_right(x):
    return pltpu.roll(x, 1, 1)


def from_right(x):
    return pltpu.roll(x, NX - 1, 1)


def mean(a, b):
    return 0.5 * (a + b)


def along_x(plus, minus):
    return minus + plus - to_right(plus) - from_right(minus)


def plane_kernel(line, own, table, base, grad, weight, single):
    v = [line[p] for p in range(5)]
    put_columns(grad, 0, [v[1], v[2]])
    put_columns(grad, 1, [v[0], v[4]])
    put_columns(single, 0, [v[3]])
    ax = [mean(own[r], from_right(own[r])) for r in range(5)]
    ay = [mean(own[r], own[r + 1]) for r in range(4)]
    put_weights(weight, 0, [ax[1], ax[2]])
    put_weights(weight, 1, [to_right(ax[1]), to_right(ax[2])])
    put_weights(weight, 2, [ay[1], ay[2]])
    put_weights(weight, 3, [ay[0], ay[1]])
    put_weights(weight, 4, [ay[0], ay[3]])
    put_weights(weight, 5, [ax[3]])
    put_weights(weight, 6, [to_right(ax[3])])
    put_weights(weight, 7, [ay[3]])
    put_weights(weight, 8, [ay[2]])
    xp, xm, yp, ym = sums(table, grad, 0, 2 * NX, weight, (0, 1, 2, 3))
    (edge,) = sums(table, grad, 1, 2 * NX, weight, (4,))
    xp3, xm3, yp3, ym3 = sums(table, single, 0, NX, weight, (5, 6, 7, 8))
    plus = [edge[:, :NX], yp[:, :NX], yp[:, NX:], yp3]
    minus = [None, ym[:, :NX], ym[:, NX:], ym3, edge[:, NX:]]
    xs = [None, (xp[:, :NX], xm[:, :NX]), (xp[:, NX:], xm[:, NX:]), (xp3, xm3)]
    for r in (1, 2, 3):
        image = along_x(*xs[r]) + (minus[r] + plus[r] - plus[r - 1] - minus[r + 1])
        base[r - 1] = line[4 + r] - image


def put_six(six, own, low_coef, high_coef):
    c = own[2]
    ax = mean(c, from_right(c))
    weights = (ax, to_right(ax), mean(c, own[3]), mean(own[1], c), mean(c, high_coef), mean(low_coef, c))
    for n, a in enumerate(weights):
        six[n] = a


def row_sums(odd, v, right, table, single, six, first_out, second_out):
    put_columns(single, 0, [v])
    xp, xm, yp, ym, zp, zm = sums(table, single, 0, NX, six, range(6))
    first_out[...] = jnp.where(odd, zm, zp)
    second_out[...] = jnp.where(odd, zp, zm)
    return yp, ym, right - along_x(xp, xm) - ((yp + ym) + (zp + zm))


def first_kernel(
    me, line, side_a, side_b, own, base, table, three, first_out, second_out, rest, six, grad, weight, single
):
    odd = me[1] == 1
    rows = []
    for r in range(3):
        below = jnp.where(odd, side_a[r], side_b[r])
        above = jnp.where(odd, side_b[r], side_a[r])
        v = line[r + 1]
        put_columns(grad, r, [v - below[:ROWS], above[:ROWS] - v])
        low, high = mean(below[ROWS:], own[r + 1]), mean(own[r + 1], above[ROWS:])
        put_weights(weight, r, [low, high])
        if r == 1:
            put_six(six, own, below[ROWS:], above[ROWS:])
    for r in range(3):
        (flux,) = sums(table, grad, r, 2 * NX, weight, (r,))
        image = flux[:, :NX] - flux[:, NX:]
        three[r] = line[r + 1] + RELAX * (base[r] - image)
    _, _, left = row_sums(odd, three[1], line[6], table, single, six, first_out, second_out)
    rest[...] = left


def second_kernel(three, own, table, rest, full, grad, weight):
    put_columns(grad, 0, [three[0], three[2]])
    put_weights(weight, 0, [mean(own[1], own[2]), mean(own[2], own[3])])
    (y,) = sums(table, grad, 0, 2 * NX, weight, (0,))
    full[...] = rest[...] + (y[:, :NX] + y[:, NX:])


def third_kernel(
    me, three, from_a, from_b, full, line, six, table, mid, first_out, second_out, y_up, y_down, rest, single
):
    odd = me[1] == 1
    v = three[1] + RELAX * (full[...] + (from_a[...] + from_b[...]))
    mid[...] = v
    y_up[...], y_down[...], rest[...] = row_sums(
        odd, v, line[6], table, single, six, first_out, second_out
    )


def back_kernel(mid, rest, from_a, from_b, y_up, y_down, send):
    whole = rest[...] + (from_a[...] + from_b[...])
    for b in range(NB):
        rows = slice(b * MP, (b + 1) * MP)
        send[b, 0] = mid[rows]
        send[b, 1] = whole[rows]
        send[b, 2] = y_up[rows]
        send[b, 3] = y_down[rows]


def last_kernel(got, out, residual):
    for y in range(NB):
        res = got[y, 1] + got[(y - 1) % NB, 2] + got[(y + 1) % NB, 3]
        new = got[y, 0] + RELAX * res
        residual[pl.ds(y, MB, stride=NB), :] = res[:MB]
        out[pl.ds(y, MB, stride=NB), :] = new[:MB]


def body(rhs, guess, coef, block_triples, offsets, values):
    slabs = lax.axis_size("slab")
    pairs_a = [(i, i ^ 1) for i in range(slabs) if i ^ 1 < slabs]
    pairs_b = [(i, ((i + 1) ^ 1) - 1) for i in range(1, slabs) if ((i + 1) ^ 1) - 1 < slabs]

    def swap(a, b):
        return lax.ppermute(a, "slab", pairs_a), lax.ppermute(b, "slab", pairs_b)

    def grads(tiles):
        return pltpu.VMEM((tiles, 3 * ROWS, 2 * NX), bf16)

    def weights(count):
        return pltpu.VMEM((count, CP, 2 * NX), f32)

    single = pltpu.VMEM((1, 3 * ROWS, NX), bf16)
    tile_flops = 2 * NK * ROWS * 3 * ROWS * 2 * NX
    flat = struct(ROWS, NX)
    me = jnp.stack([lax.axis_index("chaos"), lax.rem(lax.axis_index("slab"), 2)]).astype(jnp.int32)
    send = call(
        pack_kernel,
        "pack",
        struct(NB, 8, MP, NX),
        (guess.reshape(MB * NB, NX), rhs.reshape(MB * NB, NX)),
        scratch=[
            pltpu.VMEM((MB * NB, NX), f32),
            pltpu.VMEM((MB * NB, NX), f32),
            pltpu.SemaphoreType.DMA((2,)),
        ],
        specs=[HBM, HBM],
        limit=FULL,
    )
    got = lax.all_to_all(send, "chaos", 0, 0, tiled=True)
    table = call(
        table_kernel,
        "table",
        struct(NK * ROWS, 3 * ROWS, dtype=bf16),
        (block_triples.T, values.transpose(1, 2, 3, 0)),
        scratch=[
            pltpu.VMEM((NK * ROWS, ROWS), f32),
            pltpu.VMEM((2, 8, MP, 48), f32),
            pltpu.VMEM((2, CB * LIST * 8, ROWS), f32),
        ],
        specs=[SM, VM],
        cost=6 * tile_flops,
    )
    side, own, line = call(
        side_kernel,
        "side",
        (struct(3, ROWS + CP, NX), struct(5, CP, NX), struct(8, ROWS, NX)),
        (me, got, coef.reshape(NK * NB, NX), table),
        specs=[SM, VM, VM, ANY],
    )
    side_a, side_b = swap(side, side)
    base = call(
        plane_kernel,
        "plane",
        struct(3, ROWS, NX),
        (line, own, table),
        scratch=[grads(2), weights(9), single],
        cost=3 * tile_flops,
    )
    three, to_a, to_b, rest, six = call(
        first_kernel,
        "first",
        (struct(3, ROWS, NX), flat, flat, flat, struct(6, CP, NX)),
        (me, line, side_a, side_b, own, base, table),
        scratch=[grads(3), weights(3), single],
        specs=[SM] + [VM] * 6,
        cost=4 * tile_flops,
    )
    from_a, from_b = swap(to_a, to_b)
    full = call(
        second_kernel,
        "second",
        flat,
        (three, own, table, rest),
        scratch=[grads(1), weights(1)],
        cost=tile_flops,
    )
    mid, to_a, to_b, y_up, y_down, rest = call(
        third_kernel,
        "third",
        (flat,) * 6,
        (me, three, from_a, from_b, full, line, six, table),
        scratch=[single],
        specs=[SM] + [VM] * 7,
        cost=tile_flops,
    )
    from_a, from_b = swap(to_a, to_b)
    send = call(
        back_kernel, "back", struct(NB, 4, MP, NX), (mid, rest, from_a, from_b, y_up, y_down)
    )
    got = lax.all_to_all(send, "chaos", 0, 0, tiled=True)
    out, residual = call(
        last_kernel, "last", (struct(MB * NB, NX), struct(MB * NB, NX)), (got,)
    )
    return out.reshape(rhs.shape), residual.reshape(rhs.shape)


def solution(mesh):
    field = P("chaos", "slab", None, None)
    placed = (field, field, P(None, "slab", None, None), P(), P(), P())
    return jax.shard_map(
        body, mesh=mesh, in_specs=placed, out_specs=(field, field), check_vma=False
    )
```

```python
import jax
import jax.numpy as jnp
from jax import lax
from jax.experimental import pallas as pl
from jax.experimental.pallas import tpu as pltpu
from jax.sharding import PartitionSpec as P

MB = 15
MP = 16
NB = 8
CB = 12
KC = 3
NK = 36
NTRIP = 36
LIST = 40
ROWS = NB * MP
PART = 4
CHUNK = ROWS // PART
NX = 128
CP = 40
RELAX = 0.1
f32 = jnp.float32
bf16 = jnp.bfloat16

VM = pl.BlockSpec(memory_space=pltpu.VMEM)
SM = pl.BlockSpec(memory_space=pltpu.SMEM)
ANY = pl.BlockSpec(memory_space=pl.ANY)
HBM = pl.BlockSpec(memory_space=pltpu.HBM)
LIMIT = 20 * 2**20
FULL = 60 * 2**20


def call(kernel, name, outs, ins, scratch=(), specs=None, cost=None, limit=LIMIT):
    estimate = None
    if cost is not None:
        estimate = pl.CostEstimate(flops=cost, bytes_accessed=4 * 2**20, transcendentals=0)
    return pl.pallas_call(
        kernel,
        out_shape=outs,
        in_specs=specs or [VM] * len(ins),
        out_specs=jax.tree.map(lambda _: VM, outs),
        scratch_shapes=scratch,
        compiler_params=pltpu.CompilerParams(vmem_limit_bytes=limit),
        cost_estimate=estimate,
        name=name,
    )(*ins)


def struct(*shape, dtype=f32):
    return jax.ShapeDtypeStruct(shape, dtype)


def table_kernel(trip, values, table, dense, piece, spread):
    dense[...] = jnp.zeros_like(dense)
    piece[...] = jnp.zeros_like(piece)
    first_block = lax.broadcasted_iota(jnp.int32, (LIST, ROWS), 1) < MP
    for half in range(2):
        count = min(8, MB - 8 * half)
        for k in range(CB):
            piece[half, :count, :MB, :] = values[8 * half : 8 * half + count, k]
            block = piece[half].reshape(ROWS, 48).T[:LIST]
            for q in range(8):
                y = pltpu.roll(block, (NB - q) % NB * MP, 1) if q else block
                at = pl.ds(k * LIST * 8 + q, LIST, stride=8)
                spread[half, at, :] = jnp.where(first_block, y, 0.0)

    def place(t, carry):
        out, inner, coef = trip[0, t], trip[1, t], trip[2, t]
        base = (out // 2) * (NK * CHUNK) + coef * (CB * CHUNK) + lax.rem(out, 2) * MP
        for half in range(2):
            for k in range(CB):
                x = spread[half, pl.ds(pl.multiple_of((k * LIST + t) * 8, 8), 8), :]
                at = pl.ds(pl.multiple_of(base + k * CHUNK + half * 8, 8), 8)
                dense[at, :] += pltpu.roll(x, inner * MP, 1)
        return carry

    lax.fori_loop(0, NTRIP, place, 0)

    def cut(n, carry):
        at = pl.ds(pl.multiple_of(n * ROWS, ROWS), ROWS)
        x = dense[at, :]
        high = x.astype(bf16)
        table[at, 0:128] = high
        table[at, 128:256] = high
        table[at, 256:384] = (x - high.astype(f32)).astype(bf16)
        return carry

    lax.fori_loop(0, NK, cut, 0)


def pack_kernel(guess_hbm, rhs_hbm, send, guess, rhs, sem):
    pairs = ((guess_hbm, guess), (rhs_hbm, rhs))
    copies = [pltpu.make_async_copy(a, b, sem.at[n]) for n, (a, b) in enumerate(pairs)]
    for copy in copies:
        copy.start()
    zero = jnp.zeros((1, NX), f32)
    copies[0].wait()
    for y in range(NB):
        g = jnp.concatenate([guess[pl.ds(y, MB, stride=NB), :], zero], axis=0)
        for p in range(5):
            send[(y + 2 - p) % NB, p] = g
    copies[1].wait()
    for y in range(NB):
        r = jnp.concatenate([rhs[pl.ds(y, MB, stride=NB), :], zero], axis=0)
        for p in range(3):
            send[(y + 1 - p) % NB, 5 + p] = r


def side_kernel(me, got, coef, table, side, own, rows):
    del table
    for q in range(5):
        row = lax.rem(me[0] + q + NB - 2, NB)
        c = jnp.concatenate(
            [coef[pl.ds(row, NK, stride=NB), :], jnp.zeros((CP - NK, NX), f32)], axis=0
        )
        own[q] = c
        if 1 <= q <= 3:
            side[q - 1, ROWS:, :] = c
    for q in range(8):
        for b in range(NB):
            x = got[b, q]
            rows[q, b * MP : (b + 1) * MP, :] = x
            if 1 <= q <= 3:
                side[q - 1, b * MP : (b + 1) * MP, :] = x


def put_columns(grad, tile, columns):
    for n, g in enumerate(columns):
        high = g.astype(bf16)
        low = (g - high.astype(f32)).astype(bf16)
        lanes = slice(n * NX, (n + 1) * NX)
        grad[tile, 0:128, lanes] = high
        grad[tile, 128:256, lanes] = low
        grad[tile, 256:384, lanes] = high


def put_weights(weight, place, halves):
    for n, a in enumerate(halves):
        weight[place, :, n * NX : (n + 1) * NX] = a


def sums(table, grad, tile, width, weight, places):
    rows = []
    for part in range(PART):
        w = jnp.dot(
            table[part * NK * CHUNK : (part + 1) * NK * CHUNK, :],
            grad[tile, :, :width],
            preferred_element_type=f32,
        )
        total = [jnp.zeros((CHUNK, width), f32) for _ in places]
        for k in range(NK):
            here = w[k * CHUNK : (k + 1) * CHUNK]
            for n, p in enumerate(places):
                total[n] = total[n] + weight[p, k : k + 1, :width] * here
        rows.append(total)
    return [jnp.concatenate([r[n] for r in rows], axis=0) for n in range(len(places))]


def to_right(x):
    return pltpu.roll(x, 1, 1)


def from_right(x):
    return pltpu.roll(x, NX - 1, 1)


def mean(a, b):
    return 0.5 * (a + b)


def along_x(plus, minus):
    return minus + plus - to_right(plus) - from_right(minus)


def plane_kernel(line, own, table, base, grad, weight, single):
    v = [line[p] for p in range(5)]
    put_columns(grad, 0, [v[1], v[2]])
    put_columns(grad, 1, [v[0], v[4]])
    put_columns(single, 0, [v[3]])
    ax = [mean(own[r], from_right(own[r])) for r in range(5)]
    ay = [mean(own[r], own[r + 1]) for r in range(4)]
    put_weights(weight, 0, [ax[1], ax[2]])
    put_weights(weight, 1, [to_right(ax[1]), to_right(ax[2])])
    put_weights(weight, 2, [ay[1], ay[2]])
    put_weights(weight, 3, [ay[0], ay[1]])
    put_weights(weight, 4, [ay[0], ay[3]])
    put_weights(weight, 5, [ax[3]])
    put_weights(weight, 6, [to_right(ax[3])])
    put_weights(weight, 7, [ay[3]])
    put_weights(weight, 8, [ay[2]])
    xp, xm, yp, ym = sums(table, grad, 0, 2 * NX, weight, (0, 1, 2, 3))
    (edge,) = sums(table, grad, 1, 2 * NX, weight, (4,))
    xp3, xm3, yp3, ym3 = sums(table, single, 0, NX, weight, (5, 6, 7, 8))
    plus = [edge[:, :NX], yp[:, :NX], yp[:, NX:], yp3]
    minus = [None, ym[:, :NX], ym[:, NX:], ym3, edge[:, NX:]]
    xs = [None, (xp[:, :NX], xm[:, :NX]), (xp[:, NX:], xm[:, NX:]), (xp3, xm3)]
    for r in (1, 2, 3):
        image = along_x(*xs[r]) + (minus[r] + plus[r] - plus[r - 1] - minus[r + 1])
        base[r - 1] = line[4 + r] - image


def put_six(six, own, low_coef, high_coef):
    c = own[2]
    ax = mean(c, from_right(c))
    weights = (ax, to_right(ax), mean(c, own[3]), mean(own[1], c), mean(c, high_coef), mean(low_coef, c))
    for n, a in enumerate(weights):
        six[n] = a


def row_sums(odd, v, right, table, single, six, first_out, second_out):
    put_columns(single, 0, [v])
    xp, xm, yp, ym, zp, zm = sums(table, single, 0, NX, six, range(6))
    first_out[...] = jnp.where(odd, zm, zp)
    second_out[...] = jnp.where(odd, zp, zm)
    return yp, ym, right - along_x(xp, xm) - ((yp + ym) + (zp + zm))


def new_row(odd, line, side_a, side_b, own, base, table, grad, weight, tile, r):
    below = jnp.where(odd, side_a[r], side_b[r])
    above = jnp.where(odd, side_b[r], side_a[r])
    v = line[r + 1]
    put_columns(grad, tile, [v - below[:ROWS], above[:ROWS] - v])
    low, high = mean(below[ROWS:], own[r + 1]), mean(own[r + 1], above[ROWS:])
    put_weights(weight, tile, [low, high])
    (flux,) = sums(table, grad, tile, 2 * NX, weight, (tile,))
    new = v + RELAX * (base[r] - (flux[:, :NX] - flux[:, NX:]))
    return new, below[ROWS:], above[ROWS:]


def first_kernel(
    me, line, side_a, side_b, own, base, table, one, first_out, second_out, rest, six, grad, weight, single
):
    odd = me[1] == 1
    v, low, high = new_row(odd, line, side_a, side_b, own, base, table, grad, weight, 0, 1)
    one[...] = v
    put_six(six, own, low, high)
    _, _, left = row_sums(odd, v, line[6], table, single, six, first_out, second_out)
    rest[...] = left


def second_kernel(me, line, side_a, side_b, own, base, table, rest, full, grad, weight):
    odd = me[1] == 1
    beside = [
        new_row(odd, line, side_a, side_b, own, base, table, grad, weight, n, r)[0]
        for n, r in enumerate((0, 2))
    ]
    put_columns(grad, 2, beside)
    put_weights(weight, 2, [mean(own[1], own[2]), mean(own[2], own[3])])
    (y,) = sums(table, grad, 2, 2 * NX, weight, (2,))
    full[...] = rest[...] + (y[:, :NX] + y[:, NX:])


def third_kernel(
    me, one, from_a, from_b, full, line, six, table, mid, first_out, second_out, y_up, y_down, rest, single
):
    odd = me[1] == 1
    v = one[...] + RELAX * (full[...] + (from_a[...] + from_b[...]))
    mid[...] = v
    y_up[...], y_down[...], rest[...] = row_sums(
        odd, v, line[6], table, single, six, first_out, second_out
    )


def back_kernel(mid, rest, from_a, from_b, y_up, y_down, send):
    whole = rest[...] + (from_a[...] + from_b[...])
    for b in range(NB):
        rows = slice(b * MP, (b + 1) * MP)
        send[b, 0] = mid[rows]
        send[b, 1] = whole[rows]
        send[b, 2] = y_up[rows]
        send[b, 3] = y_down[rows]


def last_kernel(got, out, residual):
    for y in range(NB):
        res = got[y, 1] + got[(y - 1) % NB, 2] + got[(y + 1) % NB, 3]
        new = got[y, 0] + RELAX * res
        residual[pl.ds(y, MB, stride=NB), :] = res[:MB]
        out[pl.ds(y, MB, stride=NB), :] = new[:MB]


def body(rhs, guess, coef, block_triples, offsets, values):
    slabs = lax.axis_size("slab")
    pairs_a = [(i, i ^ 1) for i in range(slabs) if i ^ 1 < slabs]
    pairs_b = [(i, ((i + 1) ^ 1) - 1) for i in range(1, slabs) if ((i + 1) ^ 1) - 1 < slabs]

    def swap(a, b):
        return lax.ppermute(a, "slab", pairs_a), lax.ppermute(b, "slab", pairs_b)

    def grads(tiles):
        return pltpu.VMEM((tiles, 3 * ROWS, 2 * NX), bf16)

    def weights(count):
        return pltpu.VMEM((count, CP, 2 * NX), f32)

    single = pltpu.VMEM((1, 3 * ROWS, NX), bf16)
    tile_flops = 2 * NK * ROWS * 3 * ROWS * 2 * NX
    flat = struct(ROWS, NX)
    me = jnp.stack([lax.axis_index("chaos"), lax.rem(lax.axis_index("slab"), 2)]).astype(jnp.int32)
    send = call(
        pack_kernel,
        "pack",
        struct(NB, 8, MP, NX),
        (guess.reshape(MB * NB, NX), rhs.reshape(MB * NB, NX)),
        scratch=[
            pltpu.VMEM((MB * NB, NX), f32),
            pltpu.VMEM((MB * NB, NX), f32),
            pltpu.SemaphoreType.DMA((2,)),
        ],
        specs=[HBM, HBM],
        limit=FULL,
    )
    got = lax.all_to_all(send, "chaos", 0, 0, tiled=True)
    table = call(
        table_kernel,
        "table",
        struct(NK * ROWS, 3 * ROWS, dtype=bf16),
        (block_triples.T, values.transpose(1, 2, 3, 0)),
        scratch=[
            pltpu.VMEM((NK * ROWS, ROWS), f32),
            pltpu.VMEM((2, 8, MP, 48), f32),
            pltpu.VMEM((2, CB * LIST * 8, ROWS), f32),
        ],
        specs=[SM, VM],
        cost=6 * tile_flops,
    )
    side, own, line = call(
        side_kernel,
        "side",
        (struct(3, ROWS + CP, NX), struct(5, CP, NX), struct(8, ROWS, NX)),
        (me, got, coef.reshape(NK * NB, NX), table),
        specs=[SM, VM, VM, ANY],
    )
    side_a, side_b = swap(side, side)
    base = call(
        plane_kernel,
        "plane",
        struct(3, ROWS, NX),
        (line, own, table),
        scratch=[grads(2), weights(9), single],
        cost=3 * tile_flops,
    )
    one, to_a, to_b, rest, six = call(
        first_kernel,
        "first",
        (flat, flat, flat, flat, struct(6, CP, NX)),
        (me, line, side_a, side_b, own, base, table),
        scratch=[grads(1), weights(1), single],
        specs=[SM] + [VM] * 6,
        cost=2 * tile_flops,
    )
    from_a, from_b = swap(to_a, to_b)
    full = call(
        second_kernel,
        "second",
        flat,
        (me, line, side_a, side_b, own, base, table, rest),
        scratch=[grads(3), weights(3)],
        specs=[SM] + [VM] * 7,
        cost=3 * tile_flops,
    )
    mid, to_a, to_b, y_up, y_down, rest = call(
        third_kernel,
        "third",
        (flat,) * 6,
        (me, one, from_a, from_b, full, line, six, table),
        scratch=[single],
        specs=[SM] + [VM] * 7,
        cost=tile_flops,
    )
    from_a, from_b = swap(to_a, to_b)
    send = call(
        back_kernel, "back", struct(NB, 4, MP, NX), (mid, rest, from_a, from_b, y_up, y_down)
    )
    got = lax.all_to_all(send, "chaos", 0, 0, tiled=True)
    out, residual = call(
        last_kernel, "last", (struct(MB * NB, NX), struct(MB * NB, NX)), (got,)
    )
    return out.reshape(rhs.shape), residual.reshape(rhs.shape)


def solution(mesh):
    field = P("chaos", "slab", None, None)
    placed = (field, field, P(None, "slab", None, None), P(), P(), P())
    return jax.shard_map(
        body, mesh=mesh, in_specs=placed, out_specs=(field, field), check_vma=False
    )
```

```python
import jax
import jax.numpy as jnp
from jax import lax
from jax.experimental import pallas as pl
from jax.experimental.pallas import tpu as pltpu
from jax.sharding import PartitionSpec as P

MB = 15
MP = 16
NB = 8
CB = 12
KC = 3
NK = 36
NTRIP = 36
LIST = 40
ROWS = NB * MP
PART = 4
CHUNK = ROWS // PART
NX = 128
CP = 40
RELAX = 0.1
f32 = jnp.float32
bf16 = jnp.bfloat16

VM = pl.BlockSpec(memory_space=pltpu.VMEM)
SM = pl.BlockSpec(memory_space=pltpu.SMEM)
ANY = pl.BlockSpec(memory_space=pl.ANY)
HBM = pl.BlockSpec(memory_space=pltpu.HBM)
LIMIT = 20 * 2**20
FULL = 60 * 2**20


def call(kernel, name, outs, ins, scratch=(), specs=None, cost=None, limit=LIMIT):
    estimate = None
    if cost is not None:
        estimate = pl.CostEstimate(flops=cost, bytes_accessed=4 * 2**20, transcendentals=0)
    return pl.pallas_call(
        kernel,
        out_shape=outs,
        in_specs=specs or [VM] * len(ins),
        out_specs=jax.tree.map(lambda _: VM, outs),
        scratch_shapes=scratch,
        compiler_params=pltpu.CompilerParams(vmem_limit_bytes=limit),
        cost_estimate=estimate,
        name=name,
    )(*ins)


def struct(*shape, dtype=f32):
    return jax.ShapeDtypeStruct(shape, dtype)


def table_kernel(trip, values, table, dense, piece, spread):
    dense[...] = jnp.zeros_like(dense)
    piece[...] = jnp.zeros_like(piece)
    first_block = lax.broadcasted_iota(jnp.int32, (LIST, ROWS), 1) < MP
    for half in range(2):
        count = min(8, MB - 8 * half)
        for k in range(CB):
            piece[half, :count, :MB, :] = values[8 * half : 8 * half + count, k]
            block = piece[half].reshape(ROWS, 48).T[:LIST]
            for q in range(8):
                y = pltpu.roll(block, (NB - q) % NB * MP, 1) if q else block
                at = pl.ds(k * LIST * 8 + q, LIST, stride=8)
                spread[half, at, :] = jnp.where(first_block, y, 0.0)

    def place(t, carry):
        out, inner, coef = trip[0, t], trip[1, t], trip[2, t]
        base = (out // 2) * (NK * CHUNK) + coef * (CB * CHUNK) + lax.rem(out, 2) * MP
        for half in range(2):
            for k in range(CB):
                x = spread[half, pl.ds(pl.multiple_of((k * LIST + t) * 8, 8), 8), :]
                at = pl.ds(pl.multiple_of(base + k * CHUNK + half * 8, 8), 8)
                dense[at, :] += pltpu.roll(x, inner * MP, 1)
        return carry

    lax.fori_loop(0, NTRIP, place, 0)

    def cut(n, carry):
        at = pl.ds(pl.multiple_of(n * ROWS, ROWS), ROWS)
        x = dense[at, :]
        high = x.astype(bf16)
        table[at, 0:128] = high
        table[at, 128:256] = high
        table[at, 256:384] = (x - high.astype(f32)).astype(bf16)
        return carry

    lax.fori_loop(0, NK, cut, 0)


def pack_kernel(guess_hbm, rhs_hbm, send, guess, rhs, sem):
    pairs = ((guess_hbm, guess), (rhs_hbm, rhs))
    copies = [pltpu.make_async_copy(a, b, sem.at[n]) for n, (a, b) in enumerate(pairs)]
    for copy in copies:
        copy.start()
    zero = jnp.zeros((1, NX), f32)
    copies[0].wait()
    for y in range(NB):
        g = jnp.concatenate([guess[pl.ds(y, MB, stride=NB), :], zero], axis=0)
        for p in range(5):
            send[(y + 2 - p) % NB, p] = g
    copies[1].wait()
    for y in range(NB):
        r = jnp.concatenate([rhs[pl.ds(y, MB, stride=NB), :], zero], axis=0)
        for p in range(3):
            send[(y + 1 - p) % NB, 5 + p] = r


def side_kernel(me, got, coef, table, side, own, rows):
    del table
    for q in range(5):
        row = lax.rem(me[0] + q + NB - 2, NB)
        c = jnp.concatenate(
            [coef[pl.ds(row, NK, stride=NB), :], jnp.zeros((CP - NK, NX), f32)], axis=0
        )
        own[q] = c
        if 1 <= q <= 3:
            side[q - 1, ROWS:, :] = c
    for q in range(8):
        for b in range(NB):
            x = got[b, q]
            rows[q, b * MP : (b + 1) * MP, :] = x
            if 1 <= q <= 3:
                side[q - 1, b * MP : (b + 1) * MP, :] = x


def put_columns(grad, tile, columns):
    for n, g in enumerate(columns):
        high = g.astype(bf16)
        low = (g - high.astype(f32)).astype(bf16)
        lanes = slice(n * NX, (n + 1) * NX)
        grad[tile, 0:128, lanes] = high
        grad[tile, 128:256, lanes] = low
        grad[tile, 256:384, lanes] = high


def put_weights(weight, place, halves):
    for n, a in enumerate(halves):
        weight[place, :, n * NX : (n + 1) * NX] = a


def sums(table, grad, tile, width, weight, places):
    rows = []
    for part in range(PART):
        w = jnp.dot(
            table[part * NK * CHUNK : (part + 1) * NK * CHUNK, :],
            grad[tile, :, :width],
            preferred_element_type=f32,
        )
        total = [jnp.zeros((CHUNK, width), f32) for _ in places]
        for k in range(NK):
            here = w[k * CHUNK : (k + 1) * CHUNK]
            for n, p in enumerate(places):
                total[n] = total[n] + weight[p, k : k + 1, :width] * here
        rows.append(total)
    return [jnp.concatenate([r[n] for r in rows], axis=0) for n in range(len(places))]


def to_right(x):
    return pltpu.roll(x, 1, 1)


def from_right(x):
    return pltpu.roll(x, NX - 1, 1)


def mean(a, b):
    return 0.5 * (a + b)


def along_x(plus, minus):
    return minus + plus - to_right(plus) - from_right(minus)


def plane_kernel(line, own, table, base, grad, weight, single):
    v = [line[p] for p in range(5)]
    put_columns(grad, 0, [v[1], v[2]])
    put_columns(grad, 1, [v[0], v[4]])
    put_columns(single, 0, [v[3]])
    ax = [mean(own[r], from_right(own[r])) for r in range(5)]
    ay = [mean(own[r], own[r + 1]) for r in range(4)]
    put_weights(weight, 0, [ax[1], ax[2]])
    put_weights(weight, 1, [to_right(ax[1]), to_right(ax[2])])
    put_weights(weight, 2, [ay[1], ay[2]])
    put_weights(weight, 3, [ay[0], ay[1]])
    put_weights(weight, 4, [ay[0], ay[3]])
    put_weights(weight, 5, [ax[3]])
    put_weights(weight, 6, [to_right(ax[3])])
    put_weights(weight, 7, [ay[3]])
    put_weights(weight, 8, [ay[2]])
    xp, xm, yp, ym = sums(table, grad, 0, 2 * NX, weight, (0, 1, 2, 3))
    (edge,) = sums(table, grad, 1, 2 * NX, weight, (4,))
    xp3, xm3, yp3, ym3 = sums(table, single, 0, NX, weight, (5, 6, 7, 8))
    plus = [edge[:, :NX], yp[:, :NX], yp[:, NX:], yp3]
    minus = [None, ym[:, :NX], ym[:, NX:], ym3, edge[:, NX:]]
    xs = [None, (xp[:, :NX], xm[:, :NX]), (xp[:, NX:], xm[:, NX:]), (xp3, xm3)]
    for r in (1, 2, 3):
        image = along_x(*xs[r]) + (minus[r] + plus[r] - plus[r - 1] - minus[r + 1])
        base[r - 1] = line[4 + r] - image


def put_six(six, own, low_coef, high_coef):
    c = own[2]
    ax = mean(c, from_right(c))
    weights = (ax, to_right(ax), mean(c, own[3]), mean(own[1], c), mean(c, high_coef), mean(low_coef, c))
    for n, a in enumerate(weights):
        six[n] = a


def row_sums(odd, v, right, table, single, six, first_out, second_out):
    put_columns(single, 0, [v])
    xp, xm, yp, ym, zp, zm = sums(table, single, 0, NX, six, range(6))
    first_out[...] = jnp.where(odd, zm, zp)
    second_out[...] = jnp.where(odd, zp, zm)
    return yp, ym, right - along_x(xp, xm) - ((yp + ym) + (zp + zm))


def new_row(odd, line, side_a, side_b, own, base, table, grad, weight, tile, r):
    below = jnp.where(odd, side_a[r], side_b[r])
    above = jnp.where(odd, side_b[r], side_a[r])
    v = line[r + 1]
    put_columns(grad, tile, [v - below[:ROWS], above[:ROWS] - v])
    low, high = mean(below[ROWS:], own[r + 1]), mean(own[r + 1], above[ROWS:])
    put_weights(weight, tile, [low, high])
    (flux,) = sums(table, grad, tile, 2 * NX, weight, (tile,))
    new = v + RELAX * (base[r] - (flux[:, :NX] - flux[:, NX:]))
    return new, below[ROWS:], above[ROWS:]


def first_kernel(
    me, line, side_a, side_b, own, base, table, one, first_out, second_out, rest, six, grad, weight, single
):
    odd = me[1] == 1
    v, low, high = new_row(odd, line, side_a, side_b, own, base, table, grad, weight, 0, 1)
    one[...] = v
    put_six(six, own, low, high)
    _, _, left = row_sums(odd, v, line[6], table, single, six, first_out, second_out)
    rest[...] = left


def second_kernel(me, line, side_a, side_b, own, base, table, rest, full, grad, weight):
    odd = me[1] == 1
    beside = [
        new_row(odd, line, side_a, side_b, own, base, table, grad, weight, n, r)[0]
        for n, r in enumerate((0, 2))
    ]
    put_columns(grad, 2, beside)
    put_weights(weight, 2, [mean(own[1], own[2]), mean(own[2], own[3])])
    (y,) = sums(table, grad, 2, 2 * NX, weight, (2,))
    full[...] = rest[...] + (y[:, :NX] + y[:, NX:])


def third_kernel(
    me, one, from_a, from_b, full, line, six, table, mid, first_out, second_out, y_up, y_down, rest, single
):
    odd = me[1] == 1
    v = one[...] + RELAX * (full[...] + (from_a[...] + from_b[...]))
    mid[...] = v
    y_up[...], y_down[...], rest[...] = row_sums(
        odd, v, line[6], table, single, six, first_out, second_out
    )


def back_kernel(mid, rest, from_a, from_b, y_up, y_down, send):
    whole = rest[...] + (from_a[...] + from_b[...])
    for b in range(NB):
        rows = slice(b * MP, (b + 1) * MP)
        send[b, 0] = mid[rows]
        send[b, 1] = whole[rows]
        send[b, 2] = y_up[rows]
        send[b, 3] = y_down[rows]


def last_kernel(got, out, residual):
    for y in range(NB):
        res = got[y, 1] + got[(y - 1) % NB, 2] + got[(y + 1) % NB, 3]
        new = got[y, 0] + RELAX * res
        residual[pl.ds(y, MB, stride=NB), :] = res[:MB]
        out[pl.ds(y, MB, stride=NB), :] = new[:MB]


def body(rhs, guess, coef, block_triples, offsets, values):
    slabs = lax.axis_size("slab")
    pairs_a = [(i, i ^ 1) for i in range(slabs) if i ^ 1 < slabs]
    pairs_b = [(i, ((i + 1) ^ 1) - 1) for i in range(1, slabs) if ((i + 1) ^ 1) - 1 < slabs]

    def swap(a, b):
        b = lax.ppermute(b, "slab", pairs_b)
        return lax.ppermute(a, "slab", pairs_a), b

    def grads(tiles):
        return pltpu.VMEM((tiles, 3 * ROWS, 2 * NX), bf16)

    def weights(count):
        return pltpu.VMEM((count, CP, 2 * NX), f32)

    single = pltpu.VMEM((1, 3 * ROWS, NX), bf16)
    tile_flops = 2 * NK * ROWS * 3 * ROWS * 2 * NX
    flat = struct(ROWS, NX)
    me = jnp.stack([lax.axis_index("chaos"), lax.rem(lax.axis_index("slab"), 2)]).astype(jnp.int32)
    send = call(
        pack_kernel,
        "pack",
        struct(NB, 8, MP, NX),
        (guess.reshape(MB * NB, NX), rhs.reshape(MB * NB, NX)),
        scratch=[
            pltpu.VMEM((MB * NB, NX), f32),
            pltpu.VMEM((MB * NB, NX), f32),
            pltpu.SemaphoreType.DMA((2,)),
        ],
        specs=[HBM, HBM],
        limit=FULL,
    )
    got = lax.all_to_all(send, "chaos", 0, 0, tiled=True)
    table = call(
        table_kernel,
        "table",
        struct(NK * ROWS, 3 * ROWS, dtype=bf16),
        (block_triples.T, values.transpose(1, 2, 3, 0)),
        scratch=[
            pltpu.VMEM((NK * ROWS, ROWS), f32),
            pltpu.VMEM((2, 8, MP, 48), f32),
            pltpu.VMEM((2, CB * LIST * 8, ROWS), f32),
        ],
        specs=[SM, VM],
        cost=6 * tile_flops,
    )
    side, own, line = call(
        side_kernel,
        "side",
        (struct(3, ROWS + CP, NX), struct(5, CP, NX), struct(8, ROWS, NX)),
        (me, got, coef.reshape(NK * NB, NX), table),
        specs=[SM, VM, VM, ANY],
    )
    side_a, side_b = swap(side, side)
    base = call(
        plane_kernel,
        "plane",
        struct(3, ROWS, NX),
        (line, own, table),
        scratch=[grads(2), weights(9), single],
        cost=3 * tile_flops,
    )
    one, to_a, to_b, rest, six = call(
        first_kernel,
        "first",
        (flat, flat, flat, flat, struct(6, CP, NX)),
        (me, line, side_a, side_b, own, base, table),
        scratch=[grads(1), weights(1), single],
        specs=[SM] + [VM] * 6,
        cost=2 * tile_flops,
    )
    from_a, from_b = swap(to_a, to_b)
    full = call(
        second_kernel,
        "second",
        flat,
        (me, line, side_a, side_b, own, base, table, rest),
        scratch=[grads(3), weights(3)],
        specs=[SM] + [VM] * 7,
        cost=3 * tile_flops,
    )
    mid, to_a, to_b, y_up, y_down, rest = call(
        third_kernel,
        "third",
        (flat,) * 6,
        (me, one, from_b, from_a, full, line, six, table),
        scratch=[single],
        specs=[SM] + [VM] * 7,
        cost=tile_flops,
    )
    from_a, from_b = swap(to_a, to_b)
    send = call(
        back_kernel, "back", struct(NB, 4, MP, NX), (mid, rest, from_b, from_a, y_up, y_down)
    )
    got = lax.all_to_all(send, "chaos", 0, 0, tiled=True)
    out, residual = call(
        last_kernel, "last", (struct(MB * NB, NX), struct(MB * NB, NX)), (got,)
    )
    return out.reshape(rhs.shape), residual.reshape(rhs.shape)


def solution(mesh):
    field = P("chaos", "slab", None, None)
    placed = (field, field, P(None, "slab", None, None), P(), P(), P())
    return jax.shard_map(
        body, mesh=mesh, in_specs=placed, out_specs=(field, field), check_vma=False
    )
```

```python
import jax
import jax.numpy as jnp
from jax import lax
from jax.experimental import pallas as pl
from jax.experimental.pallas import tpu as pltpu
from jax.sharding import PartitionSpec as P

MB = 15
MP = 16
NB = 8
CB = 12
KC = 3
NK = 36
NTRIP = 36
LIST = 40
ROWS = NB * MP
PART = 4
CHUNK = ROWS // PART
NX = 128
CP = 40
RELAX = 0.1
f32 = jnp.float32
bf16 = jnp.bfloat16

VM = pl.BlockSpec(memory_space=pltpu.VMEM)
SM = pl.BlockSpec(memory_space=pltpu.SMEM)
ANY = pl.BlockSpec(memory_space=pl.ANY)
HBM = pl.BlockSpec(memory_space=pltpu.HBM)
LIMIT = 20 * 2**20
FULL = 60 * 2**20


def call(kernel, name, outs, ins, scratch=(), specs=None, cost=None, limit=LIMIT):
    estimate = None
    if cost is not None:
        estimate = pl.CostEstimate(flops=cost, bytes_accessed=4 * 2**20, transcendentals=0)
    return pl.pallas_call(
        kernel,
        out_shape=outs,
        in_specs=specs or [VM] * len(ins),
        out_specs=jax.tree.map(lambda _: VM, outs),
        scratch_shapes=scratch,
        compiler_params=pltpu.CompilerParams(vmem_limit_bytes=limit),
        cost_estimate=estimate,
        name=name,
    )(*ins)


def struct(*shape, dtype=f32):
    return jax.ShapeDtypeStruct(shape, dtype)


def table_kernel(trip, values, table, dense, piece, spread):
    dense[...] = jnp.zeros_like(dense)
    piece[...] = jnp.zeros_like(piece)
    first_block = lax.broadcasted_iota(jnp.int32, (LIST, ROWS), 1) < MP
    for half in range(2):
        count = min(8, MB - 8 * half)
        for k in range(CB):
            piece[half, :count, :MB, :] = values[8 * half : 8 * half + count, k]
            block = piece[half].reshape(ROWS, 48).T[:LIST]
            for q in range(8):
                y = pltpu.roll(block, (NB - q) % NB * MP, 1) if q else block
                at = pl.ds(k * LIST * 8 + q, LIST, stride=8)
                spread[half, at, :] = jnp.where(first_block, y, 0.0)

    def place(t, carry):
        out, inner, coef = trip[0, t], trip[1, t], trip[2, t]
        base = (out // 2) * (NK * CHUNK) + coef * (CB * CHUNK) + lax.rem(out, 2) * MP
        for half in range(2):
            for k in range(CB):
                x = spread[half, pl.ds(pl.multiple_of((k * LIST + t) * 8, 8), 8), :]
                at = pl.ds(pl.multiple_of(base + k * CHUNK + half * 8, 8), 8)
                dense[at, :] += pltpu.roll(x, inner * MP, 1)
        return carry

    lax.fori_loop(0, NTRIP, place, 0)

    def cut(n, carry):
        at = pl.ds(pl.multiple_of(n * ROWS, ROWS), ROWS)
        x = dense[at, :]
        high = x.astype(bf16)
        table[at, 0:128] = high
        table[at, 128:256] = high
        table[at, 256:384] = (x - high.astype(f32)).astype(bf16)
        return carry

    lax.fori_loop(0, NK, cut, 0)


def pack_kernel(guess_hbm, rhs_hbm, send, guess, rhs, sem):
    pairs = ((guess_hbm, guess), (rhs_hbm, rhs))
    copies = [pltpu.make_async_copy(a, b, sem.at[n]) for n, (a, b) in enumerate(pairs)]
    for copy in copies:
        copy.start()
    zero = jnp.zeros((1, NX), f32)
    copies[0].wait()
    for y in range(NB):
        g = jnp.concatenate([guess[pl.ds(y, MB, stride=NB), :], zero], axis=0)
        for p in range(5):
            send[(y + 2 - p) % NB, p] = g
    copies[1].wait()
    for y in range(NB):
        r = jnp.concatenate([rhs[pl.ds(y, MB, stride=NB), :], zero], axis=0)
        for p in range(3):
            send[(y + 1 - p) % NB, 5 + p] = r


def side_kernel(me, got, coef, table, side, own, rows):
    del table
    for q in range(5):
        row = lax.rem(me[0] + q + NB - 2, NB)
        c = jnp.concatenate(
            [coef[pl.ds(row, NK, stride=NB), :], jnp.zeros((CP - NK, NX), f32)], axis=0
        )
        own[q] = c
        if 1 <= q <= 3:
            side[q - 1, ROWS:, :] = c
    for q in range(8):
        for b in range(NB):
            x = got[b, q]
            rows[q, b * MP : (b + 1) * MP, :] = x
            if 1 <= q <= 3:
                side[q - 1, b * MP : (b + 1) * MP, :] = x


def put_columns(grad, tile, columns):
    for n, g in enumerate(columns):
        high = g.astype(bf16)
        low = (g - high.astype(f32)).astype(bf16)
        lanes = slice(n * NX, (n + 1) * NX)
        grad[tile, 0:128, lanes] = high
        grad[tile, 128:256, lanes] = low
        grad[tile, 256:384, lanes] = high


def put_weights(weight, place, halves):
    for n, a in enumerate(halves):
        weight[place, :, n * NX : (n + 1) * NX] = a


def sums(table, grad, tile, width, weight, places):
    rows = []
    for part in range(PART):
        w = jnp.dot(
            table[part * NK * CHUNK : (part + 1) * NK * CHUNK, :],
            grad[tile, :, :width],
            preferred_element_type=f32,
        )
        total = [jnp.zeros((CHUNK, width), f32) for _ in places]
        for k in range(NK):
            here = w[k * CHUNK : (k + 1) * CHUNK]
            for n, p in enumerate(places):
                total[n] = total[n] + weight[p, k : k + 1, :width] * here
        rows.append(total)
    return [jnp.concatenate([r[n] for r in rows], axis=0) for n in range(len(places))]


def to_right(x):
    return pltpu.roll(x, 1, 1)


def from_right(x):
    return pltpu.roll(x, NX - 1, 1)


def mean(a, b):
    return 0.5 * (a + b)


def along_x(plus, minus):
    return minus + plus - to_right(plus) - from_right(minus)


def plane_kernel(line, own, table, base, grad, weight, single):
    v = [line[p] for p in range(5)]
    put_columns(grad, 0, [v[1], v[2]])
    put_columns(grad, 1, [v[0], v[4]])
    put_columns(single, 0, [v[3]])
    ax = [mean(own[r], from_right(own[r])) for r in range(5)]
    ay = [mean(own[r], own[r + 1]) for r in range(4)]
    put_weights(weight, 0, [ax[1], ax[2]])
    put_weights(weight, 1, [to_right(ax[1]), to_right(ax[2])])
    put_weights(weight, 2, [ay[1], ay[2]])
    put_weights(weight, 3, [ay[0], ay[1]])
    put_weights(weight, 4, [ay[0], ay[3]])
    put_weights(weight, 5, [ax[3]])
    put_weights(weight, 6, [to_right(ax[3])])
    put_weights(weight, 7, [ay[3]])
    put_weights(weight, 8, [ay[2]])
    xp, xm, yp, ym = sums(table, grad, 0, 2 * NX, weight, (0, 1, 2, 3))
    (edge,) = sums(table, grad, 1, 2 * NX, weight, (4,))
    xp3, xm3, yp3, ym3 = sums(table, single, 0, NX, weight, (5, 6, 7, 8))
    plus = [edge[:, :NX], yp[:, :NX], yp[:, NX:], yp3]
    minus = [None, ym[:, :NX], ym[:, NX:], ym3, edge[:, NX:]]
    xs = [None, (xp[:, :NX], xm[:, :NX]), (xp[:, NX:], xm[:, NX:]), (xp3, xm3)]
    for r in (1, 2, 3):
        image = along_x(*xs[r]) + (minus[r] + plus[r] - plus[r - 1] - minus[r + 1])
        base[r - 1] = line[4 + r] - image


def put_six(six, own, low_coef, high_coef):
    c = own[2]
    ax = mean(c, from_right(c))
    weights = (ax, to_right(ax), mean(c, own[3]), mean(own[1], c), mean(c, high_coef), mean(low_coef, c))
    for n, a in enumerate(weights):
        six[n] = a


def row_sums(odd, v, right, table, single, six, first_out, second_out):
    put_columns(single, 0, [v])
    xp, xm, yp, ym, zp, zm = sums(table, single, 0, NX, six, range(6))
    first_out[...] = jnp.where(odd, zm, zp)
    second_out[...] = jnp.where(odd, zp, zm)
    return yp, ym, right - along_x(xp, xm) - ((yp + ym) + (zp + zm))


def new_row(odd, line, side_a, side_b, own, base, table, grad, weight, tile, r):
    below = jnp.where(odd, side_a[r], side_b[r])
    above = jnp.where(odd, side_b[r], side_a[r])
    v = line[r + 1]
    put_columns(grad, tile, [v - below[:ROWS], above[:ROWS] - v])
    low, high = mean(below[ROWS:], own[r + 1]), mean(own[r + 1], above[ROWS:])
    put_weights(weight, tile, [low, high])
    (flux,) = sums(table, grad, tile, 2 * NX, weight, (tile,))
    new = v + RELAX * (base[r] - (flux[:, :NX] - flux[:, NX:]))
    return new, below[ROWS:], above[ROWS:]


def first_kernel(
    me, line, side_a, side_b, own, base, table, one, first_out, second_out, rest, six, grad, weight, single
):
    odd = me[1] == 1
    v, low, high = new_row(odd, line, side_a, side_b, own, base, table, grad, weight, 0, 1)
    one[...] = v
    put_six(six, own, low, high)
    _, _, left = row_sums(odd, v, line[6], table, single, six, first_out, second_out)
    rest[...] = left


def second_kernel(me, line, side_a, side_b, own, base, table, rest, full, grad, weight):
    odd = me[1] == 1
    beside = [
        new_row(odd, line, side_a, side_b, own, base, table, grad, weight, n, r)[0]
        for n, r in enumerate((0, 2))
    ]
    put_columns(grad, 2, beside)
    put_weights(weight, 2, [mean(own[1], own[2]), mean(own[2], own[3])])
    (y,) = sums(table, grad, 2, 2 * NX, weight, (2,))
    full[...] = rest[...] + (y[:, :NX] + y[:, NX:])


def third_kernel(me, one, from_a, from_b, full, six, table, mid, first_out, second_out, single):
    odd = me[1] == 1
    v = one[...] + RELAX * (full[...] + (from_a[...] + from_b[...]))
    mid[...] = v
    put_columns(single, 0, [v])
    zp, zm = sums(table, single, 0, NX, six, (4, 5))
    first_out[...] = jnp.where(odd, zm, zp)
    second_out[...] = jnp.where(odd, zp, zm)


def fourth_kernel(mid, to_a, to_b, line, six, table, y_up, y_down, rest, single):
    put_columns(single, 0, [mid[...]])
    xp, xm, yp, ym = sums(table, single, 0, NX, six, (0, 1, 2, 3))
    y_up[...] = yp
    y_down[...] = ym
    rest[...] = line[6] - along_x(xp, xm) - ((yp + ym) + (to_a[...] + to_b[...]))


def back_kernel(mid, rest, from_a, from_b, y_up, y_down, send):
    whole = rest[...] + (from_a[...] + from_b[...])
    for b in range(NB):
        rows = slice(b * MP, (b + 1) * MP)
        send[b, 0] = mid[rows]
        send[b, 1] = whole[rows]
        send[b, 2] = y_up[rows]
        send[b, 3] = y_down[rows]


def last_kernel(got, out, residual):
    for y in range(NB):
        res = got[y, 1] + got[(y - 1) % NB, 2] + got[(y + 1) % NB, 3]
        new = got[y, 0] + RELAX * res
        residual[pl.ds(y, MB, stride=NB), :] = res[:MB]
        out[pl.ds(y, MB, stride=NB), :] = new[:MB]


def body(rhs, guess, coef, block_triples, offsets, values):
    slabs = lax.axis_size("slab")
    pairs_a = [(i, i ^ 1) for i in range(slabs) if i ^ 1 < slabs]
    pairs_b = [(i, ((i + 1) ^ 1) - 1) for i in range(1, slabs) if ((i + 1) ^ 1) - 1 < slabs]

    def swap(a, b):
        b = lax.ppermute(b, "slab", pairs_b)
        return lax.ppermute(a, "slab", pairs_a), b

    def grads(tiles):
        return pltpu.VMEM((tiles, 3 * ROWS, 2 * NX), bf16)

    def weights(count):
        return pltpu.VMEM((count, CP, 2 * NX), f32)

    single = pltpu.VMEM((1, 3 * ROWS, NX), bf16)
    tile_flops = 2 * NK * ROWS * 3 * ROWS * 2 * NX
    flat = struct(ROWS, NX)
    me = jnp.stack([lax.axis_index("chaos"), lax.rem(lax.axis_index("slab"), 2)]).astype(jnp.int32)
    send = call(
        pack_kernel,
        "pack",
        struct(NB, 8, MP, NX),
        (guess.reshape(MB * NB, NX), rhs.reshape(MB * NB, NX)),
        scratch=[
            pltpu.VMEM((MB * NB, NX), f32),
            pltpu.VMEM((MB * NB, NX), f32),
            pltpu.SemaphoreType.DMA((2,)),
        ],
        specs=[HBM, HBM],
        limit=FULL,
    )
    got = lax.all_to_all(send, "chaos", 0, 0, tiled=True)
    table = call(
        table_kernel,
        "table",
        struct(NK * ROWS, 3 * ROWS, dtype=bf16),
        (block_triples.T, values.transpose(1, 2, 3, 0)),
        scratch=[
            pltpu.VMEM((NK * ROWS, ROWS), f32),
            pltpu.VMEM((2, 8, MP, 48), f32),
            pltpu.VMEM((2, CB * LIST * 8, ROWS), f32),
        ],
        specs=[SM, VM],
        cost=6 * tile_flops,
    )
    side, own, line = call(
        side_kernel,
        "side",
        (struct(3, ROWS + CP, NX), struct(5, CP, NX), struct(8, ROWS, NX)),
        (me, got, coef.reshape(NK * NB, NX), table),
        specs=[SM, VM, VM, ANY],
    )
    side_a, side_b = swap(side, side)
    base = call(
        plane_kernel,
        "plane",
        struct(3, ROWS, NX),
        (line, own, table),
        scratch=[grads(2), weights(9), single],
        cost=3 * tile_flops,
    )
    one, to_a, to_b, rest, six = call(
        first_kernel,
        "first",
        (flat, flat, flat, flat, struct(6, CP, NX)),
        (me, line, side_a, side_b, own, base, table),
        scratch=[grads(1), weights(1), single],
        specs=[SM] + [VM] * 6,
        cost=2 * tile_flops,
    )
    from_a, from_b = swap(to_a, to_b)
    full = call(
        second_kernel,
        "second",
        flat,
        (me, line, side_a, side_b, own, base, table, rest),
        scratch=[grads(3), weights(3)],
        specs=[SM] + [VM] * 7,
        cost=3 * tile_flops,
    )
    mid, to_a, to_b = call(
        third_kernel,
        "third",
        (flat,) * 3,
        (me, one, from_b, from_a, full, six, table),
        scratch=[single],
        specs=[SM] + [VM] * 6,
        cost=tile_flops,
    )
    from_a, from_b = swap(to_a, to_b)
    y_up, y_down, rest = call(
        fourth_kernel,
        "fourth",
        (flat,) * 3,
        (mid, to_b, to_a, line, six, table),
        scratch=[single],
        cost=tile_flops,
    )
    send = call(
        back_kernel, "back", struct(NB, 4, MP, NX), (mid, rest, from_b, from_a, y_up, y_down)
    )
    got = lax.all_to_all(send, "chaos", 0, 0, tiled=True)
    out, residual = call(
        last_kernel, "last", (struct(MB * NB, NX), struct(MB * NB, NX)), (got,)
    )
    return out.reshape(rhs.shape), residual.reshape(rhs.shape)


def solution(mesh):
    field = P("chaos", "slab", None, None)
    placed = (field, field, P(None, "slab", None, None), P(), P(), P())
    return jax.shard_map(
        body, mesh=mesh, in_specs=placed, out_specs=(field, field), check_vma=False
    )
```

```python
import jax
import jax.numpy as jnp
from jax import lax
from jax.experimental import pallas as pl
from jax.experimental.pallas import tpu as pltpu
from jax.sharding import PartitionSpec as P

MB = 15
MP = 16
NB = 8
CB = 12
KC = 3
NK = 36
NTRIP = 36
LIST = 40
ROWS = NB * MP
PART = 4
CHUNK = ROWS // PART
NX = 128
CP = 40
RELAX = 0.1
f32 = jnp.float32
bf16 = jnp.bfloat16

VM = pl.BlockSpec(memory_space=pltpu.VMEM)
SM = pl.BlockSpec(memory_space=pltpu.SMEM)
ANY = pl.BlockSpec(memory_space=pl.ANY)
HBM = pl.BlockSpec(memory_space=pltpu.HBM)
LIMIT = 20 * 2**20
FULL = 60 * 2**20


def call(kernel, name, outs, ins, scratch=(), specs=None, cost=None, limit=LIMIT):
    estimate = None
    if cost is not None:
        estimate = pl.CostEstimate(flops=cost, bytes_accessed=4 * 2**20, transcendentals=0)
    return pl.pallas_call(
        kernel,
        out_shape=outs,
        in_specs=specs or [VM] * len(ins),
        out_specs=jax.tree.map(lambda _: VM, outs),
        scratch_shapes=scratch,
        compiler_params=pltpu.CompilerParams(vmem_limit_bytes=limit),
        cost_estimate=estimate,
        name=name,
    )(*ins)


def struct(*shape, dtype=f32):
    return jax.ShapeDtypeStruct(shape, dtype)


def table_kernel(trip, values, table, dense, piece, spread):
    dense[...] = jnp.zeros_like(dense)
    piece[...] = jnp.zeros_like(piece)
    first_block = lax.broadcasted_iota(jnp.int32, (LIST, ROWS), 1) < MP
    for half in range(2):
        count = min(8, MB - 8 * half)
        for k in range(CB):
            piece[half, :count, :MB, :] = values[8 * half : 8 * half + count, k]
            block = piece[half].reshape(ROWS, 48).T[:LIST]
            for q in range(8):
                y = pltpu.roll(block, (NB - q) % NB * MP, 1) if q else block
                at = pl.ds(k * LIST * 8 + q, LIST, stride=8)
                spread[half, at, :] = jnp.where(first_block, y, 0.0)

    def place(t, carry):
        out, inner, coef = trip[0, t], trip[1, t], trip[2, t]
        base = (out // 2) * (NK * CHUNK) + coef * (CB * CHUNK) + lax.rem(out, 2) * MP
        for half in range(2):
            for k in range(CB):
                x = spread[half, pl.ds(pl.multiple_of((k * LIST + t) * 8, 8), 8), :]
                at = pl.ds(pl.multiple_of(base + k * CHUNK + half * 8, 8), 8)
                dense[at, :] += pltpu.roll(x, inner * MP, 1)
        return carry

    lax.fori_loop(0, NTRIP, place, 0)

    def cut(n, carry):
        at = pl.ds(pl.multiple_of(n * ROWS, ROWS), ROWS)
        x = dense[at, :]
        high = x.astype(bf16)
        table[at, 0:128] = high
        table[at, 128:256] = high
        table[at, 256:384] = (x - high.astype(f32)).astype(bf16)
        return carry

    lax.fori_loop(0, NK, cut, 0)


def pack_kernel(guess_hbm, rhs_hbm, send, guess, rhs, sem):
    pairs = ((guess_hbm, guess), (rhs_hbm, rhs))
    copies = [pltpu.make_async_copy(a, b, sem.at[n]) for n, (a, b) in enumerate(pairs)]
    for copy in copies:
        copy.start()
    zero = jnp.zeros((1, NX), f32)
    copies[0].wait()
    for y in range(NB):
        g = jnp.concatenate([guess[pl.ds(y, MB, stride=NB), :], zero], axis=0)
        for p in range(5):
            send[(y + 2 - p) % NB, p] = g
    copies[1].wait()
    for y in range(NB):
        r = jnp.concatenate([rhs[pl.ds(y, MB, stride=NB), :], zero], axis=0)
        for p in range(3):
            send[(y + 1 - p) % NB, 5 + p] = r


def side_kernel(me, got, coef, table, side, own):
    del table
    for q in range(5):
        row = lax.rem(me[0] + q + NB - 2, NB)
        c = jnp.concatenate(
            [coef[pl.ds(row, NK, stride=NB), :], jnp.zeros((CP - NK, NX), f32)], axis=0
        )
        own[q] = c
        if 1 <= q <= 3:
            side[q - 1, ROWS:, :] = c
    for q in range(1, 4):
        for b in range(NB):
            side[q - 1, b * MP : (b + 1) * MP, :] = got[b, q]


def line_kernel(got, rows):
    for q in range(8):
        for b in range(NB):
            rows[q, b * MP : (b + 1) * MP, :] = got[b, q]


def put_columns(grad, tile, columns):
    for n, g in enumerate(columns):
        high = g.astype(bf16)
        low = (g - high.astype(f32)).astype(bf16)
        lanes = slice(n * NX, (n + 1) * NX)
        grad[tile, 0:128, lanes] = high
        grad[tile, 128:256, lanes] = low
        grad[tile, 256:384, lanes] = high


def put_weights(weight, place, halves):
    for n, a in enumerate(halves):
        weight[place, :, n * NX : (n + 1) * NX] = a


def sums(table, grad, tile, width, weight, places):
    rows = []
    for part in range(PART):
        w = jnp.dot(
            table[part * NK * CHUNK : (part + 1) * NK * CHUNK, :],
            grad[tile, :, :width],
            preferred_element_type=f32,
        )
        total = [jnp.zeros((CHUNK, width), f32) for _ in places]
        for k in range(NK):
            here = w[k * CHUNK : (k + 1) * CHUNK]
            for n, p in enumerate(places):
                total[n] = total[n] + weight[p, k : k + 1, :width] * here
        rows.append(total)
    return [jnp.concatenate([r[n] for r in rows], axis=0) for n in range(len(places))]


def to_right(x):
    return pltpu.roll(x, 1, 1)


def from_right(x):
    return pltpu.roll(x, NX - 1, 1)


def mean(a, b):
    return 0.5 * (a + b)


def along_x(plus, minus):
    return minus + plus - to_right(plus) - from_right(minus)


def plane_kernel(line, own, table, base, grad, weight, single):
    v = [line[p] for p in range(5)]
    put_columns(grad, 0, [v[1], v[2]])
    put_columns(grad, 1, [v[0], v[4]])
    put_columns(single, 0, [v[3]])
    ax = [mean(own[r], from_right(own[r])) for r in range(5)]
    ay = [mean(own[r], own[r + 1]) for r in range(4)]
    put_weights(weight, 0, [ax[1], ax[2]])
    put_weights(weight, 1, [to_right(ax[1]), to_right(ax[2])])
    put_weights(weight, 2, [ay[1], ay[2]])
    put_weights(weight, 3, [ay[0], ay[1]])
    put_weights(weight, 4, [ay[0], ay[3]])
    put_weights(weight, 5, [ax[3]])
    put_weights(weight, 6, [to_right(ax[3])])
    put_weights(weight, 7, [ay[3]])
    put_weights(weight, 8, [ay[2]])
    xp, xm, yp, ym = sums(table, grad, 0, 2 * NX, weight, (0, 1, 2, 3))
    (edge,) = sums(table, grad, 1, 2 * NX, weight, (4,))
    xp3, xm3, yp3, ym3 = sums(table, single, 0, NX, weight, (5, 6, 7, 8))
    plus = [edge[:, :NX], yp[:, :NX], yp[:, NX:], yp3]
    minus = [None, ym[:, :NX], ym[:, NX:], ym3, edge[:, NX:]]
    xs = [None, (xp[:, :NX], xm[:, :NX]), (xp[:, NX:], xm[:, NX:]), (xp3, xm3)]
    for r in (1, 2, 3):
        image = along_x(*xs[r]) + (minus[r] + plus[r] - plus[r - 1] - minus[r + 1])
        base[r - 1] = line[4 + r] - image


def put_six(six, own, low_coef, high_coef):
    c = own[2]
    ax = mean(c, from_right(c))
    weights = (ax, to_right(ax), mean(c, own[3]), mean(own[1], c), mean(c, high_coef), mean(low_coef, c))
    for n, a in enumerate(weights):
        six[n] = a


def row_sums(odd, v, right, table, single, six, first_out, second_out):
    put_columns(single, 0, [v])
    xp, xm, yp, ym, zp, zm = sums(table, single, 0, NX, six, range(6))
    first_out[...] = jnp.where(odd, zm, zp)
    second_out[...] = jnp.where(odd, zp, zm)
    return yp, ym, right - along_x(xp, xm) - ((yp + ym) + (zp + zm))


def new_row(odd, line, side_a, side_b, own, base, table, grad, weight, tile, r):
    below = jnp.where(odd, side_a[r], side_b[r])
    above = jnp.where(odd, side_b[r], side_a[r])
    v = line[r + 1]
    put_columns(grad, tile, [v - below[:ROWS], above[:ROWS] - v])
    low, high = mean(below[ROWS:], own[r + 1]), mean(own[r + 1], above[ROWS:])
    put_weights(weight, tile, [low, high])
    (flux,) = sums(table, grad, tile, 2 * NX, weight, (tile,))
    new = v + RELAX * (base[r] - (flux[:, :NX] - flux[:, NX:]))
    return new, below[ROWS:], above[ROWS:]


def first_kernel(
    me, line, side_a, side_b, own, base, table, one, first_out, second_out, rest, six, grad, weight, single
):
    odd = me[1] == 1
    v, low, high = new_row(odd, line, side_a, side_b, own, base, table, grad, weight, 0, 1)
    one[...] = v
    put_six(six, own, low, high)
    _, _, left = row_sums(odd, v, line[6], table, single, six, first_out, second_out)
    rest[...] = left


def second_kernel(me, line, side_a, side_b, own, base, table, rest, full, grad, weight):
    odd = me[1] == 1
    beside = [
        new_row(odd, line, side_a, side_b, own, base, table, grad, weight, n, r)[0]
        for n, r in enumerate((0, 2))
    ]
    put_columns(grad, 2, beside)
    put_weights(weight, 2, [mean(own[1], own[2]), mean(own[2], own[3])])
    (y,) = sums(table, grad, 2, 2 * NX, weight, (2,))
    full[...] = rest[...] + (y[:, :NX] + y[:, NX:])


def third_kernel(me, one, from_a, from_b, full, six, table, mid, first_out, second_out, single):
    odd = me[1] == 1
    v = one[...] + RELAX * (full[...] + (from_a[...] + from_b[...]))
    mid[...] = v
    put_columns(single, 0, [v])
    zp, zm = sums(table, single, 0, NX, six, (4, 5))
    first_out[...] = jnp.where(odd, zm, zp)
    second_out[...] = jnp.where(odd, zp, zm)


def fourth_kernel(mid, to_a, to_b, line, six, table, y_up, y_down, rest, single):
    put_columns(single, 0, [mid[...]])
    xp, xm, yp, ym = sums(table, single, 0, NX, six, (0, 1, 2, 3))
    y_up[...] = yp
    y_down[...] = ym
    rest[...] = line[6] - along_x(xp, xm) - ((yp + ym) + (to_a[...] + to_b[...]))


def back_kernel(mid, rest, from_a, from_b, y_up, y_down, send):
    whole = rest[...] + (from_a[...] + from_b[...])
    for b in range(NB):
        rows = slice(b * MP, (b + 1) * MP)
        send[b, 0] = mid[rows]
        send[b, 1] = whole[rows]
        send[b, 2] = y_up[rows]
        send[b, 3] = y_down[rows]


def last_kernel(got, out, residual):
    for y in range(NB):
        res = got[y, 1] + got[(y - 1) % NB, 2] + got[(y + 1) % NB, 3]
        new = got[y, 0] + RELAX * res
        residual[pl.ds(y, MB, stride=NB), :] = res[:MB]
        out[pl.ds(y, MB, stride=NB), :] = new[:MB]


def body(rhs, guess, coef, block_triples, offsets, values):
    slabs = lax.axis_size("slab")
    pairs_a = [(i, i ^ 1) for i in range(slabs) if i ^ 1 < slabs]
    pairs_b = [(i, ((i + 1) ^ 1) - 1) for i in range(1, slabs) if ((i + 1) ^ 1) - 1 < slabs]

    def swap(a, b):
        b = lax.ppermute(b, "slab", pairs_b)
        return lax.ppermute(a, "slab", pairs_a), b

    def grads(tiles):
        return pltpu.VMEM((tiles, 3 * ROWS, 2 * NX), bf16)

    def weights(count):
        return pltpu.VMEM((count, CP, 2 * NX), f32)

    single = pltpu.VMEM((1, 3 * ROWS, NX), bf16)
    tile_flops = 2 * NK * ROWS * 3 * ROWS * 2 * NX
    flat = struct(ROWS, NX)
    me = jnp.stack([lax.axis_index("chaos"), lax.rem(lax.axis_index("slab"), 2)]).astype(jnp.int32)
    send = call(
        pack_kernel,
        "pack",
        struct(NB, 8, MP, NX),
        (guess.reshape(MB * NB, NX), rhs.reshape(MB * NB, NX)),
        scratch=[
            pltpu.VMEM((MB * NB, NX), f32),
            pltpu.VMEM((MB * NB, NX), f32),
            pltpu.SemaphoreType.DMA((2,)),
        ],
        specs=[HBM, HBM],
        limit=FULL,
    )
    got = lax.all_to_all(send, "chaos", 0, 0, tiled=True)
    table = call(
        table_kernel,
        "table",
        struct(NK * ROWS, 3 * ROWS, dtype=bf16),
        (block_triples.T, values.transpose(1, 2, 3, 0)),
        scratch=[
            pltpu.VMEM((NK * ROWS, ROWS), f32),
            pltpu.VMEM((2, 8, MP, 48), f32),
            pltpu.VMEM((2, CB * LIST * 8, ROWS), f32),
        ],
        specs=[SM, VM],
        cost=6 * tile_flops,
    )
    side, own = call(
        side_kernel,
        "side",
        (struct(3, ROWS + CP, NX), struct(5, CP, NX)),
        (me, got, coef.reshape(NK * NB, NX), table),
        specs=[SM, VM, VM, ANY],
    )
    side_a, side_b = swap(side, side)
    line = call(line_kernel, "line", struct(8, ROWS, NX), (got,), cost=tile_flops)
    base = call(
        plane_kernel,
        "plane",
        struct(3, ROWS, NX),
        (line, own, table),
        scratch=[grads(2), weights(9), single],
        cost=3 * tile_flops,
    )
    one, to_a, to_b, rest, six = call(
        first_kernel,
        "first",
        (flat, flat, flat, flat, struct(6, CP, NX)),
        (me, line, side_a, side_b, own, base, table),
        scratch=[grads(1), weights(1), single],
        specs=[SM] + [VM] * 6,
        cost=2 * tile_flops,
    )
    from_a, from_b = swap(to_a, to_b)
    full = call(
        second_kernel,
        "second",
        flat,
        (me, line, side_a, side_b, own, base, table, rest),
        scratch=[grads(3), weights(3)],
        specs=[SM] + [VM] * 7,
        cost=3 * tile_flops,
    )
    mid, to_a, to_b = call(
        third_kernel,
        "third",
        (flat,) * 3,
        (me, one, from_b, from_a, full, six, table),
        scratch=[single],
        specs=[SM] + [VM] * 6,
        cost=tile_flops,
    )
    from_a, from_b = swap(to_a, to_b)
    y_up, y_down, rest = call(
        fourth_kernel,
        "fourth",
        (flat,) * 3,
        (mid, to_b, to_a, line, six, table),
        scratch=[single],
        cost=tile_flops,
    )
    send = call(
        back_kernel, "back", struct(NB, 4, MP, NX), (mid, rest, from_b, from_a, y_up, y_down)
    )
    got = lax.all_to_all(send, "chaos", 0, 0, tiled=True)
    out, residual = call(
        last_kernel, "last", (struct(MB * NB, NX), struct(MB * NB, NX)), (got,)
    )
    return out.reshape(rhs.shape), residual.reshape(rhs.shape)


def solution(mesh):
    field = P("chaos", "slab", None, None)
    placed = (field, field, P(None, "slab", None, None), P(), P(), P())
    return jax.shard_map(
        body, mesh=mesh, in_specs=placed, out_specs=(field, field), check_vma=False
    )
```
